128 devices in a mesh: gx: 16 (over x, y_hi, core), gy: 8 (over z, y_lo).
Axes of the slice: x: 4, y: 4 (y_hi: 2, y_lo: 2; y = y_hi * 2 + y_lo), z: 4, core: 2. Of those that a mesh axis runs over, the one named last changes fastest.
Arguments:
- velocity: float32 [3, 48, 64, 1024], P(None, None, 'gx', 'gy'), may hold values from -6 to 6
- stress: float32 [6, 48, 64, 1024], P(None, None, 'gx', 'gy'), may hold values from -6 to 6
- lame_lambda: float32 [48, 64, 1024], P(None, 'gx', 'gy'), may hold values from 0.5 to 2
- shear_modulus: float32 [48, 64, 1024], P(None, 'gx', 'gy'), may hold values from 0.3 to 1.5
- buoyancy: float32 [48, 64, 1024], P(None, 'gx', 'gy'), may hold values from 0.5 to 2
- water_tile: int32 [64, 1024], P('gx', 'gy'), may hold values from 0 to 65535, as said below
- water_surface: float32 [512, 8192], P('gx', 'gy'), may hold values from -6 to 6
- water_velocity: float32 [2, 512, 8192], P(None, 'gx', 'gy'), may hold values from -6 to 6
- water_depth: float32 [512, 8192], P('gx', 'gy'), may hold values from 0.5 to 2
- wet_mask: int32 [512, 8192], P('gx', 'gy'), may hold values 0 or 1
Outputs:
- final_velocity: float32 [3, 48, 64, 1024], P(None, None, 'gx', 'gy')
- final_stress: float32 [6, 48, 64, 1024], P(None, None, 'gx', 'gy')
- final_surface: float32 [512, 8192], P('gx', 'gy')
- final_flow: float32 [2, 512, 8192], P(None, 'gx', 'gy')
The draws below stay inside these ranges and needn't reach their ends.
Inputs may be any that keep to these rules, and one draw needn't show every extreme that they name: `water_tile`: every water tile is named by exactly one seafloor cell (the water model numbers its tiles in its own order, unrelated to the layout of the seafloor grid). Tile t covers water rows 8 * (t // 1024) to 8 * (t // 1024) + 7 and the like columns of t % 1024. Counting for each pair of device blocks the seafloor cells of the one that name tiles inside the water block of the other, no pair exceeds 8, and a quarter of all pairs reach exactly 8.
All inputs are finite; a program needn't handle non-finite values. No bound on the sum of `wet_mask` on one device may be relied on, other than what follows from the above.
Results may differ from the reference program's by a relative error of at most 0.00002.
Values sent between devices are 32-bit elements; how exact they have to be, the bound alone decides.
No kernel may reach another device: no remote copies, remote signals or barrier semaphores. Data moves between devices by JAX's collectives and lax.ppermute only.
A program may use at most 64 MiB of HBM per device.

```python
import math
import jax
import jax.numpy as jnp
from jax import lax

CX = 4
CY = 128
NZ = 48
TILE = 8
SEIS_STEPS = 4
WATER_STEPS = 2
NX = 64
NY = 1024
WX = 512
WY = 8192


def draw_water_tile(key, part):
    key = jax.random.fold_in(key, 7)
    grid_y = NY // CY
    devices_all = NX // CX * grid_y
    per_dev = CX * CY
    capacity = 2 * per_dev // devices_all
    keys = jax.random.split(key, 5)
    quarter = devices_all // 4
    pattern = jnp.concatenate([jnp.full((quarter,), capacity, jnp.int32), jnp.zeros((quarter,), jnp.int32), jnp.full((devices_all - 2 * quarter,), capacity // 2, jnp.int32)])
    pattern = jax.random.permutation(keys[0], pattern)
    shift_src = jax.random.permutation(keys[1], devices_all)
    shift_dst = jax.random.permutation(keys[2], devices_all)
    counts_pair = pattern[(shift_dst[None, :] - shift_src[:, None]) % devices_all]
    ends = jnp.cumsum(counts_pair, axis=1)
    offsets = jnp.cumsum(counts_pair, axis=0) - counts_pair
    positions = jnp.arange(per_dev, dtype=jnp.int32)
    target = jnp.sum((positions[None, :, None] >= ends[:, None, :]).astype(jnp.int32), axis=2)
    source_ids = jnp.arange(devices_all, dtype=jnp.int32)[:, None]
    ranking = positions[None, :] - (ends[source_ids, target] - counts_pair[source_ids, target])
    slot_at_dest = offsets[source_ids, target] + ranking
    base_rows = jnp.broadcast_to(positions[None, :], (devices_all, per_dev))
    tile_orders = jax.random.permutation(keys[3], base_rows, axis=1, independent=True)
    local_tile = tile_orders[target, slot_at_dest]
    tile_global = (target // grid_y * CX + local_tile // CY) * NY + target % grid_y * CY + local_tile % CY
    cell_orders = jax.random.permutation(keys[4], base_rows, axis=1, independent=True)
    inverse = jnp.argsort(cell_orders, axis=1)
    by_cell = jnp.take_along_axis(tile_global, inverse, axis=1)
    return by_cell.reshape(NX // CX, grid_y, CX, CY).transpose(0, 2, 1, 3).reshape(NX, NY).astype(jnp.int32)


def plant(result, rng, low, top_value):
    longest = result.shape.index(max(result.shape))
    spots = []
    for shift in (0, 1):
        where = [jax.random.randint(jax.random.fold_in(rng, axis), (), 0, length) for axis, length in enumerate(result.shape)]
        where[longest] = (where[longest] + shift) % result.shape[longest]
        spots.append(tuple(where))
    return result.at[spots[0]].set(low).at[spots[1]].set(top_value)


def level_of(rng, shape, cuts, least, top_value):
    gain = 1.0
    for axis_at, shards_of in cuts:
        heights = jax.random.uniform(jax.random.fold_in(jax.random.fold_in(rng, 6), axis_at), (shards_of,), jnp.float32, least / len(cuts), top_value / len(cuts))
        gain = gain * jnp.repeat(jnp.exp(heights), shape[axis_at] // shards_of).reshape((-1,) + (1,) * (len(shape) - 1 - axis_at))
    return gain


def scatter_about(rng, shape, scale, reach, shards=(), kind=jnp.bfloat16):
    factor_of = level_of(rng, shape, shards, -0.22, 0.18) if shards else 1.0
    drawn = jax.random.normal(rng, shape, jnp.float32) * scale * factor_of
    return jnp.minimum(jnp.maximum(drawn, -reach), reach).astype(kind)


def setup_inputs(seed: int = 0) -> dict:
    splits = jax.random.split(jax.random.key(seed), 11)
    return {
        "velocity": scatter_about(splits[0], (3, NZ, NX, NY), 1.0, 6.0, ((2, 16), (3, 8)), jnp.float32),
        "stress": scatter_about(splits[1], (6, NZ, NX, NY), 1.0, 6.0, ((2, 16), (3, 8)), jnp.float32),
        "lame_lambda": jnp.clip(jnp.exp(math.log(2.0) - 1.3862944 * jax.random.uniform(splits[2], (NZ, NX, NY), jnp.float32) ** level_of(splits[2], (NZ, NX, NY), ((1, 16), (2, 8)), -0.2, 0.2)), 0.5, 2.0),
        "shear_modulus": jnp.clip(jnp.exp(math.log(1.5) - 1.60943787 * jax.random.uniform(splits[3], (NZ, NX, NY), jnp.float32) ** level_of(splits[3], (NZ, NX, NY), ((1, 16), (2, 8)), -0.2, 0.2)), 0.3, 1.5),
        "buoyancy": jnp.clip(jnp.exp(math.log(2.0) - 1.3862944 * jax.random.uniform(splits[4], (NZ, NX, NY), jnp.float32) ** level_of(splits[4], (NZ, NX, NY), ((1, 16), (2, 8)), -0.2, 0.2)), 0.5, 2.0),
        "water_tile": draw_water_tile(jax.random.fold_in(splits[10], 71), 0),
        "water_surface": scatter_about(splits[6], (WX, WY), 1.0, 6.0, ((0, 16), (1, 8)), jnp.float32),
        "water_velocity": scatter_about(splits[7], (2, WX, WY), 1.0, 6.0, ((1, 16), (2, 8)), jnp.float32),
        "water_depth": jnp.clip(jnp.exp(math.log(2.0) - 1.3862944 * jax.random.uniform(splits[8], (WX, WY), jnp.float32) ** level_of(splits[8], (WX, WY), ((0, 16), (1, 8)), -0.2, 0.2)), 0.5, 2.0),
        "wet_mask": plant((jax.random.randint(splits[9], (WX, WY), 0, 4) < 3).astype(jnp.int32), jax.random.fold_in(splits[9], 1), 0, 1),
    }


seismic_step = 0.15
water_step = 0.4


def forward_diff(values, which_axis):
    extent = values.shape[which_axis]
    beyond = jnp.concatenate([lax.slice_in_dim(values, 1, extent, axis=which_axis), jnp.zeros_like(lax.slice_in_dim(values, 0, 1, axis=which_axis))], axis=which_axis)
    return beyond - values


def backward_diff(values, which_axis):
    extent = values.shape[which_axis]
    before = jnp.concatenate([jnp.zeros_like(lax.slice_in_dim(values, 0, 1, axis=which_axis)), lax.slice_in_dim(values, 0, extent - 1, axis=which_axis)], axis=which_axis)
    return values - before


def stress_forces(stress_now):
    force_x = forward_diff(stress_now[0], 1) + backward_diff(stress_now[3], 2) + backward_diff(stress_now[4], 0)
    force_y = backward_diff(stress_now[3], 1) + forward_diff(stress_now[1], 2) + backward_diff(stress_now[5], 0)
    force_z = backward_diff(stress_now[4], 1) + backward_diff(stress_now[5], 2) + forward_diff(stress_now[2], 0)
    return jnp.stack([force_x, force_y, force_z])


def strain_rates(motion):
    return jnp.stack([backward_diff(motion[0], 1), backward_diff(motion[1], 2), backward_diff(motion[2], 0),
                      forward_diff(motion[0], 2) + forward_diff(motion[1], 1),
                      forward_diff(motion[0], 0) + forward_diff(motion[2], 1),
                      forward_diff(motion[1], 0) + forward_diff(motion[2], 2)])


def stress_change(strain, lame_lambda, shear_modulus):
    dilation = lame_lambda * (strain[0] + strain[1] + strain[2])
    normal = dilation[None] + 2.0 * shear_modulus[None] * strain[:3]
    shear = shear_modulus[None] * strain[3:]
    return seismic_step * jnp.concatenate([normal, shear])


def water_update(surface, flow, carried):
    flow_x = flow[0] - water_step * forward_diff(surface, 0)
    flow_y = flow[1] - water_step * forward_diff(surface, 1)
    surface = surface - water_step * (backward_diff(carried * flow_x, 0) + backward_diff(carried * flow_y, 1))
    return jnp.stack([flow_x, flow_y]), surface


def reference(velocity, stress, lame_lambda, shear_modulus, buoyancy, water_tile, water_surface, water_velocity, water_depth, wet_mask):
    motion, stress_now = velocity, stress
    lift_sum = jnp.zeros((NX, NY), jnp.float32)
    for step_index in range(SEIS_STEPS):
        motion = motion + seismic_step * buoyancy[None] * stress_forces(stress_now)
        stress_now = stress_now + stress_change(strain_rates(motion), lame_lambda, shear_modulus)
        lift_sum = lift_sum + motion[2, 0]
    uplift = seismic_step * lift_sum
    tile_lift = jnp.zeros((NX * NY,), jnp.float32).at[water_tile.reshape(-1)].set(uplift.reshape(-1)).reshape(NX, NY)
    lift_cells = jnp.repeat(jnp.repeat(tile_lift, TILE, axis=0), TILE, axis=1)
    surface = water_surface + lift_cells
    flow = water_velocity
    carried = water_depth * wet_mask.astype(jnp.float32)
    for step_index in range(WATER_STEPS):
        flow, surface = water_update(surface, flow, carried)
    return motion, stress_now, surface, flow
```

```python
import functools

import jax
import jax.numpy as jnp
from jax import lax
from jax.experimental import pallas as pl
from jax.experimental.pallas import tpu as pltpu
from jax.sharding import PartitionSpec as P

SEIS_STEPS = 4
WATER_STEPS = 2

seismic_step = 0.15
water_step = 0.4

VX, VY, VZ, SXX, SYY, SZZ, SXY, SXZ, SYZ, LAM, MU, BUO = range(12)
FIELDS = 12
LANES = 128
FAR_BELOW = (VX, SXX, SXY, SXZ, BUO)
FAR_ABOVE = (VY, VZ, SXX, SYY, SZZ, SXY, SXZ, SYZ, BUO)
UP_UNITS = [(f, x) for x in range(4) for f in (FAR_BELOW if x == 0 else range(FIELDS))]
DOWN_UNITS = [(f, x) for x in range(4) for f in (FAR_ABOVE if x == 3 else range(FIELDS))]
UP_PAD = -(-len(UP_UNITS) // 3) * 3
DOWN_PAD = -(-len(DOWN_UNITS) // 3) * 3
VMEM = 48 * 1024 * 1024


def lanes_of(shape):
    return lax.broadcasted_iota(jnp.int32, shape, len(shape) - 1)


def rows_of(shape):
    return lax.broadcasted_iota(jnp.int32, shape, len(shape) - 2)


def own_row(refs, field, x, layers):
    vel, strs, lam, mu, buo = refs
    at = pl.ds(x, layers, stride=4)
    if field < 3:
        return vel[field, at, :]
    if field < 9:
        return strs[field - 3, at, :]
    return (lam, mu, buo)[field - 9][at, :]


def pack_kernel(
    layers, vel, strs, lam, mu, buo, surf, flow, depth, mask, side, near_up, near_down, far_up, far_down
):
    refs = (vel, strs, lam, mu, buo)
    half = layers // 2
    lane = lanes_of((layers, LANES))
    up_at = {unit: i for i, unit in enumerate(UP_UNITS)}
    down_at = {unit: i for i, unit in enumerate(DOWN_UNITS)}
    for tile in range(3):
        packed = jnp.zeros((layers, LANES), jnp.float32)
        for q in range(4):
            field = tile * 4 + q
            for x in range(4):
                row = own_row(refs, field, x, layers)
                for at, near, far in ((up_at, near_up, far_up), (down_at, near_down, far_down)):
                    if (field, x) in at:
                        near[at[field, x]] = row[:half]
                        far[at[field, x]] = row[half:]
                group = q * 4 + x
                packed = jnp.where(lane // 8 == group, pltpu.roll(row, (group * 8 + 4) % LANES, 1), packed)
        side[tile * layers : (tile + 1) * layers, :] = packed
    rows, cols = surf.shape
    lane = lanes_of((rows, LANES))
    packed = jnp.zeros((rows, LANES), jnp.float32)
    for f in range(4):

        def part(r0, r1, c0, c1):
            if f == 0:
                return surf[r0:r1, c0:c1]
            if f < 3:
                return flow[f - 1, r0:r1, c0:c1]
            return depth[r0:r1, c0:c1] * mask[r0:r1, c0:c1].astype(jnp.float32)

        first = pltpu.roll(part(0, rows, 0, LANES), f * 32, 1)
        last = pltpu.roll(part(0, rows, cols - LANES, cols), (f * 32 + 32) % LANES, 1)
        packed = jnp.where(lane // 2 == f * 16, first, packed)
        packed = jnp.where(lane // 2 == f * 16 + 15, last, packed)
        for c in range(cols // LANES):
            unit, row = c // 3, (c % 3) * 8 + f * 2
            near_up[UP_PAD + unit, row : row + 2, :] = part(rows - 2, rows, c * LANES, (c + 1) * LANES)
            near_down[DOWN_PAD + unit, row : row + 2, :] = part(0, 2, c * LANES, (c + 1) * LANES)
    side[3 * layers :, :] = packed


def strip_kernel(layers, own, left, right, out):
    seis = 3 * layers
    inner = lanes_of((seis, LANES)) % 8 < 4
    out[:seis, :] = jnp.where(inner, left[:seis, :], own[:seis, :])
    out[seis : 2 * seis, :] = jnp.where(inner, own[:seis, :], right[:seis, :])
    rows = own.shape[0] - seis
    low = lanes_of((rows, LANES)) % 32 < 16
    out[2 * seis :, :] = jnp.where(low, right[seis:, :], left[seis:, :])


def z_forward(f):
    n = f.shape[0]
    beyond = jnp.where(rows_of(f.shape) == n - 1, 0.0, pltpu.roll(f, n - 1, 0))
    return beyond - f


def z_backward(f):
    before = jnp.where(rows_of(f.shape) == 0, 0.0, pltpu.roll(f, 1, 0))
    return f - before


def new_velocity(vx, vy, vz, hb, sxx, sxx_xp, syy, syy_yp, szz, sxy, sxy_xm, sxy_ym, sxz, sxz_xm, syz, syz_ym):
    vx = vx + hb * ((sxx_xp - sxx) + (sxy - sxy_ym) + z_backward(sxz))
    vy = vy + hb * ((sxy - sxy_xm) + (syy_yp - syy) + z_backward(syz))
    vz = vz + hb * ((sxz - sxz_xm) + (syz - syz_ym) + z_forward(szz))
    return vx, vy, vz


def stress_gain(hl, hm, vx, vx_xm, vx_yp, vy, vy_xp, vy_ym, vz, vz_xp, vz_yp):
    ex = vx - vx_xm
    ey = vy - vy_ym
    ez = z_backward(vz)
    d = hl * (ex + ey + ez)
    twice = hm + hm
    return (
        d + twice * ex,
        d + twice * ey,
        d + twice * ez,
        hm * ((vx_yp - vx) + (vy_xp - vy)),
        hm * (z_forward(vx) + (vz_xp - vz)),
        hm * (z_forward(vy) + (vz_yp - vz)),
    )


def seismic(layers, refs, near_up, near_down, far_up, far_down, strips, below, above, state, strip, lift=None):
    lane = lanes_of((layers, LANES))
    total_layers = (strips.shape[0] - 32) // 6

    def scaled(field, value):
        return value * seismic_step if field >= LAM else value

    for field in range(FIELDS):
        for x in range(4):
            state[field, 5 + x] = scaled(field, own_row(refs, field, x, layers))
    up_at = {unit: i for i, unit in enumerate(UP_UNITS)}
    down_at = {unit: i for i, unit in enumerate(DOWN_UNITS)}
    zero = jnp.zeros((layers, LANES), jnp.float32)
    for field in range(FIELDS):
        state[field, 0] = zero
        state[field, 13] = zero
        for x in range(4):
            for at, near, far, base in ((up_at, near_up, far_up, 1), (down_at, near_down, far_down, 9)):
                if (field, x) not in at:
                    state[field, base + x] = zero
                    continue
                unit = at[field, x]
                if far is None:
                    state[field, base + x] = scaled(field, near[unit])
                else:
                    half = layers // 2
                    state[field, base + x, :half] = scaled(field, near[unit])
                    state[field, base + x, half:] = scaled(field, far[unit])
        tile, q = field // 4, field % 4
        for s in range(2):
            at = (s * 3 + tile) * total_layers
            value = jnp.where(
                lane < 32,
                pltpu.roll(below[at : at + layers, :], (-q * 32) % LANES, 1),
                jnp.where(
                    lane < 64,
                    pltpu.roll(strips[at : at + layers, :], (32 - q * 32) % LANES, 1),
                    jnp.where(lane < 96, pltpu.roll(above[at : at + layers, :], (64 - q * 32) % LANES, 1), 0.0),
                ),
            )
            strip[field, s] = scaled(field, value)

    if lift is not None:
        lift[...] = jnp.zeros_like(lift)

    def y_plus(field, value, row):
        rim = pltpu.roll(strip[field, 1], LANES - 5 - row * 8, 1)
        return jnp.where(lane == LANES - 1, rim, pltpu.roll(value, LANES - 1, 1))

    def y_minus(field, value, row):
        rim = pltpu.roll(strip[field, 0], LANES - 3 - row * 8, 1)
        return jnp.where(lane == 0, rim, pltpu.roll(value, 1, 1))

    def velocity_row(row, carry):
        at = row + 1
        sxx, syy, szz, sxy, sxz, syz = [state[f, at] for f in (SXX, SYY, SZZ, SXY, SXZ, SYZ)]
        vx, vy, vz = new_velocity(
            state[VX, at], state[VY, at], state[VZ, at], state[BUO, at],
            sxx, state[SXX, at + 1], syy, y_plus(SYY, syy, row), szz,
            sxy, state[SXY, at - 1], y_minus(SXY, sxy, row),
            sxz, state[SXZ, at - 1], syz, y_minus(SYZ, syz, row),
        )
        state[VX, at] = vx
        state[VY, at] = vy
        state[VZ, at] = vz
        return carry

    def stress_row(row, carry):
        at = row + 1
        vx, vy, vz = state[VX, at], state[VY, at], state[VZ, at]
        gains = stress_gain(
            state[LAM, at], state[MU, at],
            vx, state[VX, at - 1], y_plus(VX, vx, row),
            vy, state[VY, at + 1], y_minus(VY, vy, row),
            vz, state[VZ, at + 1], y_plus(VZ, vz, row),
        )
        for i, gain in enumerate(gains):
            state[SXX + i, at] = state[SXX + i, at] + gain
        return carry

    def y_roll(value, by):
        return pltpu.roll(value, by % LANES, 1)

    for step in range(SEIS_STEPS):
        last = step == SEIS_STEPS - 1
        if last and lift is not None:
            lax.fori_loop(4, 8, velocity_row, 0)
        else:
            lax.fori_loop(step, 12 - step, velocity_row, 0)
            for s in range(2):
                sxx, syy, szz, sxy, sxz, syz = [strip[f, s] for f in (SXX, SYY, SZZ, SXY, SXZ, SYZ)]
                new = new_velocity(
                    strip[VX, s], strip[VY, s], strip[VZ, s], strip[BUO, s],
                    sxx, y_roll(sxx, -8), syy, y_roll(syy, -1), szz,
                    sxy, y_roll(sxy, 8), y_roll(sxy, 1),
                    sxz, y_roll(sxz, 8), syz, y_roll(syz, 1),
                )
                for i in range(3):
                    strip[VX + i, s] = new[i]
        if lift is not None:
            for x in range(4):
                lift[x : x + 1, :] = lift[x : x + 1, :] + state[VZ, 5 + x, 0:1, :]
        if last and lift is not None:
            break
        lax.fori_loop(step + 1, 11 - step, stress_row, 0)
        if not last:
            for s in range(2):
                vx, vy, vz = strip[VX, s], strip[VY, s], strip[VZ, s]
                gains = stress_gain(
                    strip[LAM, s], strip[MU, s],
                    vx, y_roll(vx, 8), y_roll(vx, -1),
                    vy, y_roll(vy, -8), y_roll(vy, 1),
                    vz, y_roll(vz, -8), y_roll(vz, -1),
                )
                for i, gain in enumerate(gains):
                    strip[SXX + i, s] = strip[SXX + i, s] + gain


def full_kernel(
    layers, vel, strs, lam, mu, buo, near_up, near_down, far_up, far_down, strips, below, above, after,
    out_vel, out_strs, state, strip,
):
    seismic(
        layers, (vel, strs, lam, mu, buo), near_up, near_down, far_up, far_down, strips, below, above, state, strip
    )
    for x in range(4):
        at = pl.ds(x, layers, stride=4)
        for f in range(3):
            out_vel[f, at, :] = state[f, 5 + x]
        for f in range(6):
            out_strs[f, at, :] = state[SXX + f, 5 + x]


def three_parts(value):
    high = value.astype(jnp.bfloat16)
    rest = value - high.astype(jnp.float32)
    middle = rest.astype(jnp.bfloat16)
    low = (rest - middle.astype(jnp.float32)).astype(jnp.bfloat16)
    return high, middle, low


def lift_kernel(
    layers, grid_x, grid_y, vel, strs, lam, mu, buo, near_up, near_down, strips, below, above, tiles,
    out, state, strip, lift,
):
    seismic(layers, (vel, strs, lam, mu, buo), near_up, near_down, None, None, strips, below, above, state, strip, lift)
    cols_dev = tiles.shape[1]
    wide = grid_y * cols_dev
    reach = grid_x * 8
    tile = tiles[...]
    tile_row, tile_col = tile // wide, tile % wide
    lead = lax.broadcasted_iota(jnp.int32, (reach, cols_dev), 0)
    wanted_row = jnp.where(lead % 8 < 6, lead // 8 * 4 - 1 + lead % 8, -2)
    column = lax.broadcasted_iota(jnp.int32, (wide, cols_dev), 0)
    edge = lax.broadcasted_iota(jnp.int32, (16, cols_dev), 0)
    wanted_edge = jnp.where(edge < 2 * grid_y, edge // 2 * cols_dev + jnp.where(edge % 2 == 0, -1, cols_dev), -2)
    body = jnp.zeros((3 * reach, wide), jnp.float32)
    rim = jnp.zeros((16, 3 * reach), jnp.float32)
    contract = (((1,), (1,)), ((), ()))
    lefts, cols_hot, edges_hot = [], [], []
    for x in range(4):
        value = seismic_step * lift[x : x + 1, :]
        here = wanted_row == tile_row[x : x + 1, :]
        spread = jnp.where(here, jnp.broadcast_to(value, here.shape), 0.0)
        lefts.append(jnp.concatenate(three_parts(spread), axis=0))
        one = jnp.float32(1)
        cols_hot.append(jnp.where(column == tile_col[x : x + 1, :], one, 0.0).astype(jnp.bfloat16))
        edges_hot.append(jnp.where(wanted_edge == tile_col[x : x + 1, :], one, 0.0).astype(jnp.bfloat16))
    left = jnp.concatenate(lefts, axis=1)
    body = lax.dot_general(left, jnp.concatenate(cols_hot, axis=1), contract, preferred_element_type=jnp.float32)
    rim = lax.dot_general(jnp.concatenate(edges_hot, axis=1), left, contract, preferred_element_type=jnp.float32)
    body = body[:reach] + body[reach : 2 * reach] + body[2 * reach :]
    rim = rim[:, :reach] + rim[:, reach : 2 * reach] + rim[:, 2 * reach :]
    if reach < LANES:
        rim = jnp.concatenate([rim, jnp.zeros((16, LANES - reach), jnp.float32)], axis=1)
    row = rows_of((8, cols_dev))
    for gy in range(grid_y):
        beside = jnp.where(
            row == 6,
            jnp.broadcast_to(rim[2 * gy : 2 * gy + 1, :], (8, LANES)),
            jnp.broadcast_to(rim[2 * gy + 1 : 2 * gy + 2, :], (8, LANES)),
        )
        for gx in range(grid_x):
            block = body[gx * 8 : gx * 8 + 8, gy * cols_dev : (gy + 1) * cols_dev]
            out[gx * grid_y + gy] = jnp.where(row < 6, block, beside)


def water_kernel(
    grid_x, grid_y, place, parts, surf, flow, depth, mask, near_up, near_down, strips, below, above,
    out_surf, out_flow, ext,
):
    rows, cols = surf.shape
    tall, wide = rows + 16, cols + LANES
    me_x, me_y = place[0], place[1]
    ext[...] = jnp.zeros_like(ext)
    lift = jnp.sum(parts[...], axis=0)
    lane = lanes_of((8, LANES))
    spread = jnp.where(
        rows_of((LANES, cols)) == lanes_of((LANES, cols)) // 8, jnp.float32(1), 0.0
    ).astype(jnp.bfloat16)
    cells = jnp.dot(jnp.concatenate(three_parts(lift), axis=0), spread, preferred_element_type=jnp.float32)
    cells = cells[:8] + cells[8:16] + cells[16:]
    for f in range(4):
        for c in range(cols // LANES):
            unit, row = c // 3, (c % 3) * 8 + f * 2
            at = slice(c * LANES, (c + 1) * LANES)
            ext[f, 6:8, at] = near_up[unit, row : row + 2, :]
            ext[f, 8 + rows : 10 + rows, at] = near_down[unit, row : row + 2, :]
    ext[0, 8 : 8 + rows, :cols] = surf[...]
    ext[1, 8 : 8 + rows, :cols] = flow[0]
    ext[2, 8 : 8 + rows, :cols] = flow[1]
    ext[3, 8 : 8 + rows, :cols] = depth[...] * mask[...].astype(jnp.float32)
    rims = jnp.concatenate([below[rows - 8 : rows, :], strips[...], above[:8, :]], axis=0)
    wide_lane = lanes_of((tall, LANES))
    for f in range(4):
        after = pltpu.roll(rims, (-f * 32) % LANES, 1)
        before = pltpu.roll(rims, (96 - f * 32) % LANES, 1)
        ext[f, :, cols:] = jnp.where(wide_lane < 2, after, jnp.where(wide_lane >= LANES - 2, before, 0.0))
    for r in range(tall // 8):
        at = slice(r * 8, r * 8 + 8)
        ext[0, at, :cols] = ext[0, at, :cols] + jnp.broadcast_to(cells[r : r + 1, :], (8, cols))
        picked = jnp.sum(jnp.where(lane == me_x * 8 + r, lift, 0.0), axis=1, keepdims=True)
        left = jnp.broadcast_to(picked[6:7, :], (8, LANES))
        right = jnp.broadcast_to(picked[7:8, :], (8, LANES))
        ext[0, at, cols:] = ext[0, at, cols:] + jnp.where(
            lane < 2, right, jnp.where(lane >= LANES - 2, left, 0.0)
        )
    eta, u, w, carried = ext[0], ext[1], ext[2], ext[3]
    row, col = rows_of((tall, wide)), lanes_of((tall, wide))
    outside = jnp.logical_or(
        jnp.logical_and(me_x == grid_x - 1, row >= 8 + rows),
        jnp.logical_and(me_y == grid_y - 1, jnp.logical_and(col >= cols, col < cols + LANES // 2)),
    )
    for step in range(WATER_STEPS):
        u = u - water_step * (pltpu.roll(eta, tall - 1, 0) - eta)
        w = w - water_step * (pltpu.roll(eta, wide - 1, 1) - eta)
        cu, cw = carried * u, carried * w
        eta = eta - water_step * ((cu - pltpu.roll(cu, 1, 0)) + (cw - pltpu.roll(cw, 1, 1)))
        if step < WATER_STEPS - 1:
            eta = jnp.where(outside, 0.0, eta)
    out_surf[...] = eta[8 : 8 + rows, :cols]
    out_flow[0] = u[8 : 8 + rows, :cols]
    out_flow[1] = w[8 : 8 + rows, :cols]


def whole(shape):
    return pl.BlockSpec(shape, lambda i: (0,) * len(shape))


def call(kernel, ins, in_specs, out_shapes, scratch=(), flops=0):
    specs = [whole(a.shape) if s is None else s for a, s in zip(ins, in_specs)]
    moved = sum(4 * a.size for a in ins) + sum(4 * s.size for s in out_shapes)
    return pl.pallas_call(
        kernel,
        grid=(1,),
        in_specs=specs,
        out_specs=[whole(s.shape) for s in out_shapes],
        out_shape=list(out_shapes),
        scratch_shapes=list(scratch),
        compiler_params=pltpu.CompilerParams(vmem_limit_bytes=VMEM),
        cost_estimate=pl.CostEstimate(flops=flops, bytes_accessed=moved, transcendentals=0),
    )(*ins)


def shift(value, axis, by):
    count = lax.axis_size(axis)
    return lax.ppermute(value, axis, [(i, i + by) for i in range(count) if 0 <= i + by < count])


def f32(*shape):
    return jax.ShapeDtypeStruct(shape, jnp.float32)


def body(
    velocity, stress, lame_lambda, shear_modulus, buoyancy, water_tile, water_surface, water_velocity, water_depth, wet_mask
):
    layers, rows_dev, cols_dev = lame_lambda.shape
    grid_x, grid_y = lax.axis_size("gx"), lax.axis_size("gy")
    devices = grid_x * grid_y
    water_rows, water_cols = water_surface.shape
    flat = layers * rows_dev
    own = (
        velocity.reshape(3, flat, cols_dev),
        stress.reshape(6, flat, cols_dev),
        lame_lambda.reshape(flat, cols_dev),
        shear_modulus.reshape(flat, cols_dev),
        buoyancy.reshape(flat, cols_dev),
    )
    water = (water_surface, water_velocity, water_depth, wet_mask)
    half = layers // 2
    side, near_up, near_down, far_up, far_down = call(
        functools.partial(pack_kernel, layers),
        own + water,
        [None] * 9,
        [
            f32(3 * layers + water_rows, LANES),
            f32(UP_PAD + 3, half, LANES),
            f32(DOWN_PAD + 3, half, LANES),
            f32(len(UP_UNITS), half, LANES),
            f32(len(DOWN_UNITS), half, LANES),
        ],
    )
    left, right = shift(side, "gy", 1), shift(side, "gy", -1)
    near_up, near_down = shift(near_up, "gx", 1), shift(near_down, "gx", -1)
    (strips,) = call(
        functools.partial(strip_kernel, layers),
        (side, left, right),
        [None] * 3,
        [f32(6 * layers + water_rows, LANES)],
    )
    below, above = shift(strips, "gx", 1), shift(strips, "gx", -1)
    far_up, far_down = shift(far_up, "gx", 1), shift(far_down, "gx", -1)
    top = 8
    (send,) = call(
        functools.partial(lift_kernel, top, grid_x, grid_y),
        own + (near_up, near_down, strips, below, above, water_tile),
        [
            whole((3, top * rows_dev, cols_dev)),
            whole((6, top * rows_dev, cols_dev)),
            whole((top * rows_dev, cols_dev)),
            whole((top * rows_dev, cols_dev)),
            whole((top * rows_dev, cols_dev)),
            whole((UP_PAD + 3, top, LANES)),
            whole((DOWN_PAD + 3, top, LANES)),
            None,
            None,
            None,
            None,
        ],
        [f32(devices, 8, LANES)],
        [
            pltpu.VMEM((FIELDS, 14, top, LANES), jnp.float32),
            pltpu.VMEM((FIELDS, 2, top, LANES), jnp.float32),
            pltpu.VMEM((8, LANES), jnp.float32),
        ],
    )
    parts = lax.all_to_all(send, ("gx", "gy"), split_axis=0, concat_axis=0, tiled=True)
    place = jnp.stack([lax.axis_index("gx"), lax.axis_index("gy")]).astype(jnp.int32)
    rims = pl.BlockSpec((water_rows, LANES), lambda i: (6 * layers // water_rows, 0))
    final_surface, final_flow = call(
        functools.partial(water_kernel, grid_x, grid_y),
        (place, parts) + water + (near_up, near_down, strips, below, above),
        [
            pl.BlockSpec(memory_space=pltpu.SMEM),
            None,
            None,
            None,
            None,
            None,
            pl.BlockSpec((3, half, LANES), lambda i: (UP_PAD // 3, 0, 0)),
            pl.BlockSpec((3, half, LANES), lambda i: (DOWN_PAD // 3, 0, 0)),
            rims,
            rims,
            rims,
        ],
        [f32(water_rows, water_cols), f32(2, water_rows, water_cols)],
        [pltpu.VMEM((4, water_rows + 16, water_cols + LANES), jnp.float32)],
    )
    final_velocity, final_stress = call(
        functools.partial(full_kernel, layers),
        own + (near_up, near_down, far_up, far_down, strips, below, above, parts),
        [None] * 12 + [whole((1, 8, LANES))],
        [f32(3, flat, cols_dev), f32(6, flat, cols_dev)],
        [
            pltpu.VMEM((FIELDS, 14, layers, LANES), jnp.float32),
            pltpu.VMEM((FIELDS, 2, layers, LANES), jnp.float32),
        ],
        flops=70 * 9 * flat * cols_dev * 4,
    )
    return (
        final_velocity.reshape(velocity.shape),
        final_stress.reshape(stress.shape),
        final_surface,
        final_flow,
    )


def solution(mesh):
    placed = (
        P(None, None, "gx", "gy"),
        P(None, None, "gx", "gy"),
        P(None, "gx", "gy"),
        P(None, "gx", "gy"),
        P(None, "gx", "gy"),
        P("gx", "gy"),
        P("gx", "gy"),
        P(None, "gx", "gy"),
        P("gx", "gy"),
        P("gx", "gy"),
    )
    return jax.shard_map(
        body,
        mesh=mesh,
        in_specs=placed,
        out_specs=(
            P(None, None, "gx", "gy"),
            P(None, None, "gx", "gy"),
            P("gx", "gy"),
            P(None, "gx", "gy"),
        ),
        check_vma=False,
    )
```

```python
import functools

import jax
import jax.numpy as jnp
from jax import lax
from jax.experimental import pallas as pl
from jax.experimental.pallas import tpu as pltpu
from jax.sharding import PartitionSpec as P

SEIS_STEPS = 4
WATER_STEPS = 2

seismic_step = 0.15
water_step = 0.4

VX, VY, VZ, SXX, SYY, SZZ, SXY, SXZ, SYZ, LAM, MU, BUO = range(12)
FIELDS = 12
LANES = 128
FAR_BELOW = (VX, SXX, SXY, SXZ, BUO)
FAR_ABOVE = (VY, VZ, SXX, SYY, SZZ, SXY, SXZ, SYZ, BUO)
UP_UNITS = [(f, x) for x in range(4) for f in (FAR_BELOW if x == 0 else range(FIELDS))]
DOWN_UNITS = [(f, x) for x in range(4) for f in (FAR_ABOVE if x == 3 else range(FIELDS))]
FIRST = 20
UNITS = max(len(UP_UNITS), len(DOWN_UNITS))
VMEM = 40 * 1024 * 1024
ALL_VMEM = 62 * 1024 * 1024
TOP = 8


def lanes_of(shape):
    return lax.broadcasted_iota(jnp.int32, shape, len(shape) - 1)


def rows_of(shape):
    return lax.broadcasted_iota(jnp.int32, shape, len(shape) - 2)


def own_row(refs, field, x, layers):
    vel, strs, lam, mu, buo = refs
    at = pl.ds(x, layers, stride=4)
    if field < 3:
        return vel[field, at, :]
    if field < 9:
        return strs[field - 3, at, :]
    return (lam, mu, buo)[field - 9][at, :]


def side_kernel(layers, vel, strs, lam, mu, buo, surf, flow, depth, mask, side):
    refs = (vel, strs, lam, mu, buo)
    lane = lanes_of((layers, LANES))
    for tile in range(3):
        packed = jnp.zeros((layers, LANES), jnp.float32)
        for q in range(4):
            for x in range(4):
                row = own_row(refs, tile * 4 + q, x, layers)
                group = q * 4 + x
                packed = jnp.where(lane // 8 == group, pltpu.roll(row, (group * 8 + 4) % LANES, 1), packed)
        side[tile * layers : (tile + 1) * layers, :] = packed
    rows, cols = surf.shape
    lane = lanes_of((rows, LANES))
    packed = jnp.zeros((rows, LANES), jnp.float32)
    for f in range(4):
        first = pltpu.roll(water_part(f, surf, flow, depth, mask, 0, rows, 0, LANES), f * 32, 1)
        last = pltpu.roll(water_part(f, surf, flow, depth, mask, 0, rows, cols - LANES, cols), (f * 32 + 32) % LANES, 1)
        packed = jnp.where(lane // 2 == f * 16, first, packed)
        packed = jnp.where(lane // 2 == f * 16 + 15, last, packed)
    side[3 * layers :, :] = packed


def water_part(f, surf, flow, depth, mask, r0, r1, c0, c1):
    if f == 0:
        return surf[r0:r1, c0:c1]
    if f < 3:
        return flow[f - 1, r0:r1, c0:c1]
    return depth[r0:r1, c0:c1] * mask[r0:r1, c0:c1].astype(jnp.float32)


def rows_kernel(
    layers, odd, vel, strs, lam, mu, buo, surf, flow, depth, mask,
    side, near_in, near_out, first_in, first_out, last_in, last_out,
):
    refs = (vel, strs, lam, mu, buo)
    rows, cols = surf.shape
    base = cols // LANES * 8
    rest = layers - TOP

    side_kernel(layers, vel, strs, lam, mu, buo, surf, flow, depth, mask, side)

    def write(units, start, near, first, last):
        for f in range(4):
            for c in range(cols // LANES):
                near[c * 8 + f * 2 : c * 8 + f * 2 + 2, :] = water_part(
                    f, surf, flow, depth, mask, start, start + 2, c * LANES, (c + 1) * LANES
                )
        for unit, (field, x) in enumerate(units):
            row = own_row(refs, field, x, layers)
            near[base + unit * TOP : base + unit * TOP + TOP, :] = row[:TOP]
            if unit < FIRST:
                first[unit] = row[TOP:]
            else:
                last[(6 + unit - FIRST) * rest : (7 + unit - FIRST) * rest, :] = row[TOP:]

    @pl.when(odd[0] == 0)
    def _():
        write(UP_UNITS, rows - 2, near_in, first_in, last_in)
        write(DOWN_UNITS, 0, near_out, first_out, last_out)

    @pl.when(odd[0] == 1)
    def _():
        write(UP_UNITS, rows - 2, near_out, first_out, last_out)
        write(DOWN_UNITS, 0, near_in, first_in, last_in)


def strip_kernel(
    layers, left, right, side, near_in, near_out, last_in, last_out,
    x_in, x_out, same_side, same_near_in, same_near_out, same_in, same_out, own, low, done,
):
    rest = layers - TOP
    seis = 3 * layers
    rows = own.shape[0] - seis
    head = 6 * TOP + rows
    arriving = [pltpu.make_async_copy(side, own, done.at[0])]
    for i, (near, x_ref) in enumerate(((near_in, x_in), (near_out, x_out))):
        arriving.append(pltpu.make_async_copy(near, x_ref.at[head : x_ref.shape[0], :], done.at[1 + i]))
    for copy in arriving:
        copy.start()
    arriving[0].wait()
    inner = lanes_of((layers, LANES)) % 8 < 4
    for tile in range(3):
        at = slice(tile * layers, (tile + 1) * layers)
        mine = own[at, :]
        for edge, rim in ((0, jnp.where(inner, left[at, :], mine)), (1, jnp.where(inner, mine, right[at, :]))):
            slot = edge * 3 + tile
            low[slot * rest : (slot + 1) * rest, :] = rim[TOP:]
            for x_ref in (x_in, x_out):
                x_ref[slot * TOP : slot * TOP + TOP, :] = rim[:TOP]
    leaving = [
        pltpu.make_async_copy(low, same.at[0 : 6 * rest, :], done.at[3 + i]) for i, same in enumerate((same_in, same_out))
    ]
    for copy in leaving:
        copy.start()
    water = jnp.where(lanes_of((rows, LANES)) % 32 < 16, right[seis:, :], left[seis:, :])
    for x_ref in (x_in, x_out):
        x_ref[6 * TOP : head, :] = water
    for copy in arriving[1:] + leaving:
        copy.wait()


def after_kernel(first, last, same):
    pass


def z_forward(f):
    n = f.shape[0]
    beyond = jnp.where(rows_of(f.shape) == n - 1, 0.0, pltpu.roll(f, n - 1, 0))
    return beyond - f


def z_backward(f):
    before = jnp.where(rows_of(f.shape) == 0, 0.0, pltpu.roll(f, 1, 0))
    return f - before


def new_velocity(vx, vy, vz, hb, sxx, sxx_xp, syy, syy_yp, szz, sxy, sxy_xm, sxy_ym, sxz, sxz_xm, syz, syz_ym):
    vx = vx + hb * ((sxx_xp - sxx) + (sxy - sxy_ym) + z_backward(sxz))
    vy = vy + hb * ((sxy - sxy_xm) + (syy_yp - syy) + z_backward(syz))
    vz = vz + hb * ((sxz - sxz_xm) + (syz - syz_ym) + z_forward(szz))
    return vx, vy, vz


def stress_gain(hl, hm, vx, vx_xm, vx_yp, vy, vy_xp, vy_ym, vz, vz_xp, vz_yp):
    ex = vx - vx_xm
    ey = vy - vy_ym
    ez = z_backward(vz)
    d = hl * (ex + ey + ez)
    twice = hm + hm
    return (
        d + twice * ex,
        d + twice * ey,
        d + twice * ez,
        hm * ((vx_yp - vx) + (vy_xp - vy)),
        hm * (z_forward(vx) + (vz_xp - vz)),
        hm * (z_forward(vy) + (vz_yp - vz)),
    )


def seismic(layers, refs, rims, below, above, units, state, strip, lift=None):
    lane = lanes_of((layers, LANES))

    def scaled(field, value):
        return value * seismic_step if field >= LAM else value

    for field in range(FIELDS):
        for x in range(4):
            state[field, 5 + x] = scaled(field, own_row(refs, field, x, layers))
    up_at = {unit: i for i, unit in enumerate(UP_UNITS)}
    down_at = {unit: i for i, unit in enumerate(DOWN_UNITS)}
    zero = jnp.zeros((layers, LANES), jnp.float32)
    for field in range(FIELDS):
        state[field, 0] = zero
        state[field, 13] = zero
        for x in range(4):
            for at, side, first in ((up_at, below, 1), (down_at, above, 9)):
                if (field, x) not in at:
                    state[field, first + x] = zero
                    continue
                for layer, piece in units(side, at[field, x]):
                    state[field, first + x, layer : layer + piece.shape[0]] = scaled(field, piece)
        tile, q = field // 4, field % 4
        for s in range(2):
            low, own, high = rims(s * 3 + tile)
            value = jnp.where(
                lane < 32,
                pltpu.roll(low, (-q * 32) % LANES, 1),
                jnp.where(
                    lane < 64,
                    pltpu.roll(own, (32 - q * 32) % LANES, 1),
                    jnp.where(lane < 96, pltpu.roll(high, (64 - q * 32) % LANES, 1), 0.0),
                ),
            )
            strip[field, s] = scaled(field, value)

    if lift is not None:
        lift[...] = jnp.zeros_like(lift)

    def y_plus(field, value, row):
        rim = pltpu.roll(strip[field, 1], LANES - 5 - row * 8, 1)
        return jnp.where(lane == LANES - 1, rim, pltpu.roll(value, LANES - 1, 1))

    def y_minus(field, value, row):
        rim = pltpu.roll(strip[field, 0], LANES - 3 - row * 8, 1)
        return jnp.where(lane == 0, rim, pltpu.roll(value, 1, 1))

    def velocity_row(row):
        at = row + 1
        sxx, syy, szz, sxy, sxz, syz = [state[f, at] for f in (SXX, SYY, SZZ, SXY, SXZ, SYZ)]
        vx, vy, vz = new_velocity(
            state[VX, at], state[VY, at], state[VZ, at], state[BUO, at],
            sxx, state[SXX, at + 1], syy, y_plus(SYY, syy, row), szz,
            sxy, state[SXY, at - 1], y_minus(SXY, sxy, row),
            sxz, state[SXZ, at - 1], syz, y_minus(SYZ, syz, row),
        )
        state[VX, at] = vx
        state[VY, at] = vy
        state[VZ, at] = vz

    def stress_row(row):
        at = row + 1
        vx, vy, vz = state[VX, at], state[VY, at], state[VZ, at]
        gains = stress_gain(
            state[LAM, at], state[MU, at],
            vx, state[VX, at - 1], y_plus(VX, vx, row),
            vy, state[VY, at + 1], y_minus(VY, vy, row),
            vz, state[VZ, at + 1], y_plus(VZ, vz, row),
        )
        for i, gain in enumerate(gains):
            state[SXX + i, at] = state[SXX + i, at] + gain

    def each(first, end, update):
        for row in range(first, end):
            update(row)

    def y_roll(value, by):
        return pltpu.roll(value, by % LANES, 1)

    for step in range(SEIS_STEPS):
        last = step == SEIS_STEPS - 1
        if last and lift is not None:
            each(4, 8, velocity_row)
        else:
            each(step, 12 - step, velocity_row)
            for s in range(2):
                sxx, syy, szz, sxy, sxz, syz = [strip[f, s] for f in (SXX, SYY, SZZ, SXY, SXZ, SYZ)]
                new = new_velocity(
                    strip[VX, s], strip[VY, s], strip[VZ, s], strip[BUO, s],
                    sxx, y_roll(sxx, -8), syy, y_roll(syy, -1), szz,
                    sxy, y_roll(sxy, 8), y_roll(sxy, 1),
                    sxz, y_roll(sxz, 8), syz, y_roll(syz, 1),
                )
                for i in range(3):
                    strip[VX + i, s] = new[i]
        if lift is not None:
            for x in range(4):
                lift[x : x + 1, :] = lift[x : x + 1, :] + state[VZ, 5 + x, 0:1, :]
        if last and lift is not None:
            break
        each(step + 1, 11 - step, stress_row)
        if not last:
            for s in range(2):
                vx, vy, vz = strip[VX, s], strip[VY, s], strip[VZ, s]
                gains = stress_gain(
                    strip[LAM, s], strip[MU, s],
                    vx, y_roll(vx, 8), y_roll(vx, -1),
                    vy, y_roll(vy, -8), y_roll(vy, 1),
                    vz, y_roll(vz, -8), y_roll(vz, -1),
                )
                for i, gain in enumerate(gains):
                    strip[SXX + i, s] = strip[SXX + i, s] + gain


def sides(odd, inner, outer):
    even = odd[0] == 0

    def below(i, at):
        return jnp.where(even, outer[i][at], inner[i][at])

    def above(i, at):
        return jnp.where(even, inner[i][at], outer[i][at])

    return below, above


def full_kernel(
    layers, base, odd, vel, strs, lam, mu, buo, strips, lows, x_in, x_out, first_in, first_out, last_in, last_out,
    out_vel, out_strs, state, strip,
):
    below, above = sides(odd, (x_in, first_in, last_in), (x_out, first_out, last_out))
    rest = layers - TOP

    def units(side, unit):
        top = side(0, slice(base + unit * TOP, base + unit * TOP + TOP))
        if unit < FIRST:
            return (0, top), (TOP, side(1, unit))
        return (0, top), (TOP, side(2, slice((6 + unit - FIRST) * rest, (7 + unit - FIRST) * rest)))

    def rims(slot):
        top, low = slice(slot * TOP, slot * TOP + TOP), slice(slot * rest, (slot + 1) * rest)
        parts = (below(0, top), below(2, low)), (strips[top, :], lows[low, :]), (above(0, top), above(2, low))
        return [jnp.concatenate(p, axis=0) for p in parts]

    seismic(layers, (vel, strs, lam, mu, buo), rims, below, above, units, state, strip)
    for x in range(4):
        at = pl.ds(x, layers, stride=4)
        for f in range(3):
            out_vel[f, at, :] = state[f, 5 + x]
        for f in range(6):
            out_strs[f, at, :] = state[SXX + f, 5 + x]


def three_parts(value):
    high = value.astype(jnp.bfloat16)
    rest = value - high.astype(jnp.float32)
    middle = rest.astype(jnp.bfloat16)
    low = (rest - middle.astype(jnp.float32)).astype(jnp.bfloat16)
    return high, middle, low


def lift_kernel(
    base, grid_x, grid_y,
    odd, vel, strs, lam, mu, buo, strips, x_in, x_out, tiles, first, center, out, state, strip, lift,
):
    below, above = sides(odd, (x_in,), (x_out,))

    def units(side, unit):
        return ((0, side(0, slice(base + unit * TOP, base + unit * TOP + TOP))),)

    def rims(slot):
        top = slice(slot * TOP, slot * TOP + TOP)
        return below(0, top), strips[top, :], above(0, top)

    seismic(TOP, (vel, strs, lam, mu, buo), rims, below, above, units, state, strip, lift)
    cols_dev = tiles.shape[1]
    wide = grid_y * cols_dev
    reach = grid_x * 8
    tile = tiles[...]
    tile_row, tile_col = tile // wide, tile % wide
    lead = lax.broadcasted_iota(jnp.int32, (reach, cols_dev), 0)
    wanted_row = jnp.where(lead % 8 < 6, lead // 8 * 4 - 1 + lead % 8, -2)
    column = lax.broadcasted_iota(jnp.int32, (wide, cols_dev), 0)
    edge = lax.broadcasted_iota(jnp.int32, (16, cols_dev), 0)
    wanted_edge = jnp.where(edge < 2 * grid_y, edge // 2 * cols_dev + jnp.where(edge % 2 == 0, -1, cols_dev), -2)
    contract = (((1,), (1,)), ((), ()))
    lefts, cols_hot, edges_hot = [], [], []
    for x in range(4):
        value = seismic_step * lift[x : x + 1, :]
        here = wanted_row == tile_row[x : x + 1, :]
        spread = jnp.where(here, jnp.broadcast_to(value, here.shape), 0.0)
        lefts.append(jnp.concatenate(three_parts(spread), axis=0))
        one = jnp.float32(1)
        cols_hot.append(jnp.where(column == tile_col[x : x + 1, :], one, 0.0).astype(jnp.bfloat16))
        edges_hot.append(jnp.where(wanted_edge == tile_col[x : x + 1, :], one, 0.0).astype(jnp.bfloat16))
    left = jnp.concatenate(lefts, axis=1)
    body = lax.dot_general(left, jnp.concatenate(cols_hot, axis=1), contract, preferred_element_type=jnp.float32)
    rim = lax.dot_general(jnp.concatenate(edges_hot, axis=1), left, contract, preferred_element_type=jnp.float32)
    body = body[:reach] + body[reach : 2 * reach] + body[2 * reach :]
    rim = rim[:, :reach] + rim[:, reach : 2 * reach] + rim[:, 2 * reach :]
    if reach < LANES:
        rim = jnp.concatenate([rim, jnp.zeros((16, LANES - reach), jnp.float32)], axis=1)
    row = rows_of((8, cols_dev))
    for gy in range(grid_y):
        beside = jnp.where(
            row == 6,
            jnp.broadcast_to(rim[2 * gy : 2 * gy + 1, :], (8, LANES)),
            jnp.broadcast_to(rim[2 * gy + 1 : 2 * gy + 2, :], (8, LANES)),
        )
        for gx in range(grid_x):
            block = body[gx * 8 : gx * 8 + 8, gy * cols_dev : (gy + 1) * cols_dev]
            out[gx * grid_y + gy] = jnp.where(row < 6, block, beside)


def center_kernel(surf, flow, depth, mask, ext):
    rows, cols = surf.shape
    ext[...] = jnp.zeros_like(ext)
    ext[0, 8 : 8 + rows, :cols] = surf[...]
    ext[1, 8 : 8 + rows, :cols] = flow[0]
    ext[2, 8 : 8 + rows, :cols] = flow[1]
    ext[3, 8 : 8 + rows, :cols] = depth[...] * mask[...].astype(jnp.float32)


def border_kernel(odd, strips, x_in, x_out, center, ext):
    tall, rows, cols = ext.shape[1], ext.shape[1] - 16, ext.shape[2] - LANES
    below, above = sides(odd, (x_in,), (x_out,))
    ext[...] = center[...]
    for f in range(4):
        for c in range(cols // LANES):
            row = 6 * TOP + rows + c * 8 + f * 2
            at = slice(c * LANES, (c + 1) * LANES)
            ext[f, 6:8, at] = below(0, slice(row, row + 2))
            ext[f, 8 + rows : 10 + rows, at] = above(0, slice(row, row + 2))
    rims = jnp.concatenate(
        [
            below(0, slice(6 * TOP + rows - 8, 6 * TOP + rows)),
            strips[6 * TOP : 6 * TOP + rows, :],
            above(0, slice(6 * TOP, 6 * TOP + 8)),
        ],
        axis=0,
    )
    wide_lane = lanes_of((tall, LANES))
    for f in range(4):
        after = pltpu.roll(rims, (-f * 32) % LANES, 1)
        before = pltpu.roll(rims, (96 - f * 32) % LANES, 1)
        ext[f, :, cols:] = jnp.where(wide_lane < 2, after, jnp.where(wide_lane >= LANES - 2, before, 0.0))


def water_kernel(grid_x, grid_y, place, parts, ext, first, out_surf, out_flow):
    rows, cols = out_surf.shape
    tall, wide = rows + 16, cols + LANES
    me_x, me_y = place[0], place[1]
    lift = jnp.sum(parts[...], axis=0)
    lane = lanes_of((8, LANES))
    spread = jnp.where(
        rows_of((LANES, cols)) == lanes_of((LANES, cols)) // 8, jnp.float32(1), 0.0
    ).astype(jnp.bfloat16)
    cells = jnp.dot(jnp.concatenate(three_parts(lift), axis=0), spread, preferred_element_type=jnp.float32)
    cells = cells[:8] + cells[8:16] + cells[16:]
    surface = []
    for r in range(tall // 8):
        picked = jnp.sum(jnp.where(lane == me_x * 8 + r, lift, 0.0), axis=1, keepdims=True)
        left = jnp.broadcast_to(picked[6:7, :], (8, LANES))
        right = jnp.broadcast_to(picked[7:8, :], (8, LANES))
        beside = jnp.where(lane < 2, right, jnp.where(lane >= LANES - 2, left, 0.0))
        lifted = jnp.concatenate([jnp.broadcast_to(cells[r : r + 1, :], (8, cols)), beside], axis=1)
        surface.append(ext[0, r * 8 : r * 8 + 8, :] + lifted)
    eta, u, w, carried = jnp.concatenate(surface, axis=0), ext[1], ext[2], ext[3]
    row, col = rows_of((tall, wide)), lanes_of((tall, wide))
    outside = jnp.logical_or(
        jnp.logical_and(me_x == grid_x - 1, row >= 8 + rows),
        jnp.logical_and(me_y == grid_y - 1, jnp.logical_and(col >= cols, col < cols + LANES // 2)),
    )
    for step in range(WATER_STEPS):
        u = u - water_step * (pltpu.roll(eta, tall - 1, 0) - eta)
        w = w - water_step * (pltpu.roll(eta, wide - 1, 1) - eta)
        cu, cw = carried * u, carried * w
        eta = eta - water_step * ((cu - pltpu.roll(cu, 1, 0)) + (cw - pltpu.roll(cw, 1, 1)))
        if step < WATER_STEPS - 1:
            eta = jnp.where(outside, 0.0, eta)
    out_surf[...] = eta[8 : 8 + rows, :cols]
    out_flow[0] = u[8 : 8 + rows, :cols]
    out_flow[1] = w[8 : 8 + rows, :cols]


def whole(shape):
    return pl.BlockSpec(shape, lambda i: (0,) * len(shape))


ANYWHERE = pl.BlockSpec(memory_space=pl.ANY)


class Fetch:
    def __init__(self, rows=None):
        self.rows = rows


def call(kernel, ins, in_specs, out_shapes, scratch=(), flops=0, same=(), vmem=VMEM):
    specs, fetched, cuts = [], [], {}
    for i, (a, s) in enumerate(zip(ins, in_specs)):
        if isinstance(s, Fetch):
            shape = a.shape if s.rows is None else a.shape[:-2] + (s.rows,) + a.shape[-1:]
            cuts[i] = len(fetched), shape
            fetched.append(pltpu.VMEM(shape, a.dtype))
            specs.append(pl.BlockSpec(memory_space=pltpu.HBM))
        else:
            specs.append(whole(a.shape) if s is None else s)
    count = len(ins)

    def fetching(*refs):
        refs = list(refs)
        arrived = refs.pop()
        buffers = refs[len(refs) - len(fetched) :]
        refs = refs[: len(refs) - len(fetched)]
        copies = []
        for i, (slot, shape) in cuts.items():
            source = refs[i]
            if shape != ins[i].shape:
                source = source.at[(slice(None),) * (len(shape) - 2) + (slice(0, shape[-2]),)]
            copies.append(pltpu.make_async_copy(source, buffers[slot], arrived.at[slot]))
            refs[i] = buffers[slot]
        for copy in copies:
            copy.start()
        for copy in copies:
            copy.wait()
        kernel(*refs)

    if cuts:
        scratch = list(scratch) + fetched + [pltpu.SemaphoreType.DMA((len(fetched),))]
    moved = sum(4 * a.size for a in ins) + sum(4 * s.size for s in out_shapes)
    return pl.pallas_call(
        fetching if cuts else kernel,
        grid=(1,),
        in_specs=specs,
        out_specs=[ANYWHERE if i in dict(same).values() else whole(s.shape) for i, s in enumerate(out_shapes)],
        input_output_aliases=dict(same),
        out_shape=list(out_shapes),
        scratch_shapes=list(scratch),
        compiler_params=pltpu.CompilerParams(vmem_limit_bytes=vmem),
        cost_estimate=pl.CostEstimate(flops=flops, bytes_accessed=moved, transcendentals=0),
    )(*ins)


def shift(value, axis, by):
    count = lax.axis_size(axis)
    return lax.ppermute(value, axis, [(i, i + by) for i in range(count) if 0 <= i + by < count])


def partner(value, start):
    pairs = [(i, i + 1) for i in range(start, lax.axis_size("gx") - 1, 2)]
    return lax.ppermute(value, "gx", pairs + [(j, i) for i, j in pairs])


def f32(*shape):
    return jax.ShapeDtypeStruct(shape, jnp.float32)


def body(
    velocity, stress, lame_lambda, shear_modulus, buoyancy, water_tile, water_surface, water_velocity, water_depth, wet_mask
):
    layers, rows_dev, cols_dev = lame_lambda.shape
    grid_x, grid_y = lax.axis_size("gx"), lax.axis_size("gy")
    devices = grid_x * grid_y
    water_rows, water_cols = water_surface.shape
    flat = layers * rows_dev
    own = (
        velocity.reshape(3, flat, cols_dev),
        stress.reshape(6, flat, cols_dev),
        lame_lambda.reshape(flat, cols_dev),
        shear_modulus.reshape(flat, cols_dev),
        buoyancy.reshape(flat, cols_dev),
    )
    water = (water_surface, water_velocity, water_depth, wet_mask)
    rest = layers - TOP
    water_tiles = water_cols // LANES * 8
    base = 6 * TOP + water_rows + water_tiles
    x_shape = f32(base + UNITS * TOP, LANES)
    near_shape = f32(water_tiles + UNITS * TOP, LANES)
    first_shape = f32(FIRST, rest, LANES)
    last_shape = f32((6 + UNITS - FIRST) * rest, LANES)
    place = jnp.stack([lax.axis_index("gx"), lax.axis_index("gy")]).astype(jnp.int32)
    odd = place[:1] % 2
    smem = pl.BlockSpec(memory_space=pltpu.SMEM)
    side, near_in, near_out, first_in, first_out, last_in, last_out = call(
        functools.partial(rows_kernel, layers),
        (odd,) + own + water,
        [smem] + [Fetch()] * 9,
        [f32(3 * layers + water_rows, LANES), near_shape, near_shape, first_shape, first_shape, last_shape, last_shape],
        vmem=ALL_VMEM,
    )
    left, right = shift(side, "gy", 1), shift(side, "gy", -1)
    first_in, first_out = partner(first_in, 0), partner(first_out, 1)
    side_shape = f32(3 * layers + water_rows, LANES)
    x_own, x_out, _, _, _, last_own, last_out = call(
        functools.partial(strip_kernel, layers),
        (left, right, side, near_in, near_out, last_in, last_out),
        [None] * 2 + [ANYWHERE] * 5,
        [x_shape, x_shape, side_shape, near_shape, near_shape, last_shape, last_shape],
        [
            pltpu.VMEM(side_shape.shape, jnp.float32),
            pltpu.VMEM((6 * rest, LANES), jnp.float32),
            pltpu.SemaphoreType.DMA((5,)),
        ],
        same=((2, 2), (3, 3), (4, 4), (5, 5), (6, 6)),
    )
    x_in, x_out = partner(x_own, 0), partner(x_out, 1)
    (last_out,) = call(
        after_kernel, (x_in, last_out), [ANYWHERE] * 2, [last_shape], same=((1, 0),)
    )
    last_in, last_out = partner(last_own, 0), partner(last_out, 1)
    ext_shape = f32(4, water_rows + 16, water_cols + LANES)
    (center,) = call(center_kernel, water, [None] * 4, [ext_shape])
    (send,) = call(
        functools.partial(lift_kernel, base, grid_x, grid_y),
        (odd,) + own + (x_own, x_in, x_out, water_tile, first_out, center),
        [smem] + [None] * 9 + [ANYWHERE] * 2,
        [f32(devices, 8, LANES)],
        [
            pltpu.VMEM((FIELDS, 14, TOP, LANES), jnp.float32),
            pltpu.VMEM((FIELDS, 2, TOP, LANES), jnp.float32),
            pltpu.VMEM((8, LANES), jnp.float32),
        ],
    )
    parts = lax.all_to_all(send, ("gx", "gy"), split_axis=0, concat_axis=0, tiled=True)
    final_velocity, final_stress = call(
        functools.partial(full_kernel, layers, base),
        (odd,) + own + (x_own, last_own, x_in, x_out, first_in, first_out, last_in, last_out),
        [smem] + [None] * 13,
        [f32(3, flat, cols_dev), f32(6, flat, cols_dev)],
        [
            pltpu.VMEM((FIELDS, 14, layers, LANES), jnp.float32),
            pltpu.VMEM((FIELDS, 2, layers, LANES), jnp.float32),
        ],
        flops=70 * 9 * flat * cols_dev * 4,
    )
    (ext,) = call(border_kernel, (odd, x_own, x_in, x_out, center), [smem] + [None] * 4, [ext_shape])
    final_surface, final_flow = call(
        functools.partial(water_kernel, grid_x, grid_y),
        (place, parts, ext, final_velocity),
        [smem, None, None, ANYWHERE],
        [f32(water_rows, water_cols), f32(2, water_rows, water_cols)],
    )
    return (
        final_velocity.reshape(velocity.shape),
        final_stress.reshape(stress.shape),
        final_surface,
        final_flow,
    )


def solution(mesh):
    placed = (
        P(None, None, "gx", "gy"),
        P(None, None, "gx", "gy"),
        P(None, "gx", "gy"),
        P(None, "gx", "gy"),
        P(None, "gx", "gy"),
        P("gx", "gy"),
        P("gx", "gy"),
        P(None, "gx", "gy"),
        P("gx", "gy"),
        P("gx", "gy"),
    )
    return jax.shard_map(
        body,
        mesh=mesh,
        in_specs=placed,
        out_specs=(
            P(None, None, "gx", "gy"),
            P(None, None, "gx", "gy"),
            P("gx", "gy"),
            P(None, "gx", "gy"),
        ),
        check_vma=False,
    )
```

```python
import functools
import math

import jax
import jax.numpy as jnp
from jax import lax
from jax.experimental import pallas as pl
from jax.experimental.pallas import tpu as pltpu
from jax.sharding import PartitionSpec as P

SEIS_STEPS = 4
WATER_STEPS = 2

seismic_step = 0.15
water_step = 0.4

VX, VY, VZ, SXX, SYY, SZZ, SXY, SXZ, SYZ, LAM, MU, BUO = range(12)
FIELDS = 12
LANES = 128
FAR_BELOW = (VX, SXX, SXY, SXZ, BUO)
FAR_ABOVE = (VY, VZ, SXX, SYY, SZZ, SXY, SXZ, SYZ, BUO)
UP_UNITS = [(f, x) for x in range(4) for f in (FAR_BELOW if x == 0 else range(FIELDS))]
DOWN_UNITS = [(f, x) for x in range(4) for f in (FAR_ABOVE if x == 3 else range(FIELDS))]
FIRST = 18
UNITS = max(len(UP_UNITS), len(DOWN_UNITS))
VMEM = 48 * 1024 * 1024
ALL_VMEM = 63 * 1024 * 1024
TOP = 8


def lanes_of(shape):
    return lax.broadcasted_iota(jnp.int32, shape, len(shape) - 1)


def rows_of(shape):
    return lax.broadcasted_iota(jnp.int32, shape, len(shape) - 2)


def own_row(refs, field, x, layers):
    vel, strs, lam, mu, buo = refs
    at = pl.ds(x, layers, stride=4)
    if field < 3:
        return vel[field, at, :]
    if field < 9:
        return strs[field - 3, at, :]
    return (lam, mu, buo)[field - 9][at, :]


def side_kernel(layers, vel, strs, lam, mu, buo, surf, flow, depth, mask, side):
    refs = (vel, strs, lam, mu, buo)
    lane = lanes_of((layers, LANES))
    for tile in range(3):
        packed = jnp.zeros((layers, LANES), jnp.float32)
        for q in range(4):
            for x in range(4):
                row = own_row(refs, tile * 4 + q, x, layers)
                group = q * 4 + x
                packed = jnp.where(lane // 8 == group, pltpu.roll(row, (group * 8 + 4) % LANES, 1), packed)
        side[tile * layers : (tile + 1) * layers, :] = packed
    rows, cols = surf.shape
    lane = lanes_of((rows, LANES))
    packed = jnp.zeros((rows, LANES), jnp.float32)
    for f in range(4):
        first = pltpu.roll(water_part(f, surf, flow, depth, mask, 0, rows, 0, LANES), f * 32, 1)
        last = pltpu.roll(water_part(f, surf, flow, depth, mask, 0, rows, cols - LANES, cols), (f * 32 + 32) % LANES, 1)
        packed = jnp.where(lane // 2 == f * 16, first, packed)
        packed = jnp.where(lane // 2 == f * 16 + 15, last, packed)
    side[3 * layers :, :] = packed


def water_part(f, surf, flow, depth, mask, r0, r1, c0, c1):
    if f == 0:
        return surf[r0:r1, c0:c1]
    if f < 3:
        return flow[f - 1, r0:r1, c0:c1]
    return depth[r0:r1, c0:c1] * mask[r0:r1, c0:c1].astype(jnp.float32)


def rows_kernel(
    layers, odd, vel, strs, lam, mu, buo, surf, flow, depth, mask,
    side, near_in, near_out, first_in, first_out, last_in, last_out,
):
    refs = (vel, strs, lam, mu, buo)
    rows, cols = surf.shape
    base = cols // LANES * 8
    rest = layers - TOP
    room = last_in.shape[0] - (UNITS - FIRST) * rest

    side_kernel(layers, vel, strs, lam, mu, buo, surf, flow, depth, mask, side)

    def write(units, start, near, first, last):
        for f in range(4):
            for c in range(cols // LANES):
                first[c * 8 + f * 2 : c * 8 + f * 2 + 2, :] = water_part(
                    f, surf, flow, depth, mask, start, start + 2, c * LANES, (c + 1) * LANES
                )
        for unit, (field, x) in enumerate(units):
            row = own_row(refs, field, x, layers)
            near[unit * TOP : unit * TOP + TOP, :] = row[:TOP]
            if unit < FIRST:
                first[base + unit * rest : base + (unit + 1) * rest, :] = row[TOP:]
            else:
                last[room + (unit - FIRST) * rest : room + (unit - FIRST + 1) * rest, :] = row[TOP:]

    @pl.when(odd[0] == 0)
    def _():
        write(UP_UNITS, rows - 2, near_in, first_in, last_in)
        write(DOWN_UNITS, 0, near_out, first_out, last_out)

    @pl.when(odd[0] == 1)
    def _():
        write(UP_UNITS, rows - 2, near_out, first_out, last_out)
        write(DOWN_UNITS, 0, near_in, first_in, last_in)


def strip_kernel(
    layers, left, right, own, near_in, near_out, last_in, last_out, x_in, x_out, same_in, same_out, low, done
):
    rest = layers - TOP
    seis = 3 * layers
    inner = lanes_of((layers, LANES)) % 8 < 4
    for tile in range(3):
        at = slice(tile * layers, (tile + 1) * layers)
        mine = own[at, :]
        for edge, rim in ((0, jnp.where(inner, left[at, :], mine)), (1, jnp.where(inner, mine, right[at, :]))):
            slot = edge * 3 + tile
            low[slot * rest : (slot + 1) * rest, :] = rim[TOP:]
            for x_ref in (x_in, x_out):
                x_ref[slot * TOP : slot * TOP + TOP, :] = rim[:TOP]
    rows = own.shape[0] - seis
    low[6 * rest :, :] = jnp.where(lanes_of((rows, LANES)) % 32 < 16, right[seis:, :], left[seis:, :])
    copies = [
        pltpu.make_async_copy(low, same.at[0 : low.shape[0], :], done.at[i]) for i, same in enumerate((same_in, same_out))
    ]
    for copy in copies:
        copy.start()
    x_in[6 * TOP :, :] = near_in[...]
    x_out[6 * TOP :, :] = near_out[...]
    for copy in copies:
        copy.wait()


def after_kernel(first, last, same):
    pass


def z_forward(f):
    n = f.shape[0]
    beyond = jnp.where(rows_of(f.shape) == n - 1, 0.0, pltpu.roll(f, n - 1, 0))
    return beyond - f


def z_backward(f):
    before = jnp.where(rows_of(f.shape) == 0, 0.0, pltpu.roll(f, 1, 0))
    return f - before


def new_velocity(vx, vy, vz, hb, sxx, sxx_xp, syy, syy_yp, szz, sxy, sxy_xm, sxy_ym, sxz, sxz_xm, syz, syz_ym):
    vx = vx + hb * ((sxx_xp - sxx) + (sxy - sxy_ym) + z_backward(sxz))
    vy = vy + hb * ((sxy - sxy_xm) + (syy_yp - syy) + z_backward(syz))
    vz = vz + hb * ((sxz - sxz_xm) + (syz - syz_ym) + z_forward(szz))
    return vx, vy, vz


def stress_gain(hl, hm, vx, vx_xm, vx_yp, vy, vy_xp, vy_ym, vz, vz_xp, vz_yp):
    ex = vx - vx_xm
    ey = vy - vy_ym
    ez = z_backward(vz)
    d = hl * (ex + ey + ez)
    twice = hm + hm
    return (
        d + twice * ex,
        d + twice * ey,
        d + twice * ez,
        hm * ((vx_yp - vx) + (vy_xp - vy)),
        hm * (z_forward(vx) + (vz_xp - vz)),
        hm * (z_forward(vy) + (vz_yp - vz)),
    )


def seismic(layers, refs, rims, below, above, units, state, strip, lift=None):
    lane = lanes_of((layers, LANES))

    def scaled(field, value):
        return value * seismic_step if field >= LAM else value

    for field in range(FIELDS):
        for x in range(4):
            state[field, 5 + x] = scaled(field, own_row(refs, field, x, layers))
    up_at = {unit: i for i, unit in enumerate(UP_UNITS)}
    down_at = {unit: i for i, unit in enumerate(DOWN_UNITS)}
    zero = jnp.zeros((layers, LANES), jnp.float32)
    for field in range(FIELDS):
        state[field, 0] = zero
        state[field, 13] = zero
        for x in range(4):
            for at, side, first in ((up_at, below, 1), (down_at, above, 9)):
                if (field, x) not in at:
                    state[field, first + x] = zero
                    continue
                for layer, piece in units(side, at[field, x]):
                    state[field, first + x, layer : layer + piece.shape[0]] = scaled(field, piece)
        tile, q = field // 4, field % 4
        for s in range(2):
            low, own, high = rims(s * 3 + tile)
            value = jnp.where(
                lane < 32,
                pltpu.roll(low, (-q * 32) % LANES, 1),
                jnp.where(
                    lane < 64,
                    pltpu.roll(own, (32 - q * 32) % LANES, 1),
                    jnp.where(lane < 96, pltpu.roll(high, (64 - q * 32) % LANES, 1), 0.0),
                ),
            )
            strip[field, s] = scaled(field, value)

    if lift is not None:
        lift[...] = jnp.zeros_like(lift)

    def y_plus(field, value, row):
        rim = pltpu.roll(strip[field, 1], LANES - 5 - row * 8, 1)
        return jnp.where(lane == LANES - 1, rim, pltpu.roll(value, LANES - 1, 1))

    def y_minus(field, value, row):
        rim = pltpu.roll(strip[field, 0], LANES - 3 - row * 8, 1)
        return jnp.where(lane == 0, rim, pltpu.roll(value, 1, 1))

    def velocity_row(row):
        at = row + 1
        sxx, syy, szz, sxy, sxz, syz = [state[f, at] for f in (SXX, SYY, SZZ, SXY, SXZ, SYZ)]
        vx, vy, vz = new_velocity(
            state[VX, at], state[VY, at], state[VZ, at], state[BUO, at],
            sxx, state[SXX, at + 1], syy, y_plus(SYY, syy, row), szz,
            sxy, state[SXY, at - 1], y_minus(SXY, sxy, row),
            sxz, state[SXZ, at - 1], syz, y_minus(SYZ, syz, row),
        )
        state[VX, at] = vx
        state[VY, at] = vy
        state[VZ, at] = vz

    def stress_row(row):
        at = row + 1
        vx, vy, vz = state[VX, at], state[VY, at], state[VZ, at]
        gains = stress_gain(
            state[LAM, at], state[MU, at],
            vx, state[VX, at - 1], y_plus(VX, vx, row),
            vy, state[VY, at + 1], y_minus(VY, vy, row),
            vz, state[VZ, at + 1], y_plus(VZ, vz, row),
        )
        for i, gain in enumerate(gains):
            state[SXX + i, at] = state[SXX + i, at] + gain

    def each(first, end, update):
        for row in range(first, end):
            update(row)

    def y_roll(value, by):
        return pltpu.roll(value, by % LANES, 1)

    for step in range(SEIS_STEPS):
        last = step == SEIS_STEPS - 1
        if last and lift is not None:
            each(4, 8, velocity_row)
        else:
            each(step, 12 - step, velocity_row)
            for s in range(2):
                sxx, syy, szz, sxy, sxz, syz = [strip[f, s] for f in (SXX, SYY, SZZ, SXY, SXZ, SYZ)]
                new = new_velocity(
                    strip[VX, s], strip[VY, s], strip[VZ, s], strip[BUO, s],
                    sxx, y_roll(sxx, -8), syy, y_roll(syy, -1), szz,
                    sxy, y_roll(sxy, 8), y_roll(sxy, 1),
                    sxz, y_roll(sxz, 8), syz, y_roll(syz, 1),
                )
                for i in range(3):
                    strip[VX + i, s] = new[i]
        if lift is not None:
            for x in range(4):
                lift[x : x + 1, :] = lift[x : x + 1, :] + state[VZ, 5 + x, 0:1, :]
        if last and lift is not None:
            break
        each(step + 1, 11 - step, stress_row)
        if not last:
            for s in range(2):
                vx, vy, vz = strip[VX, s], strip[VY, s], strip[VZ, s]
                gains = stress_gain(
                    strip[LAM, s], strip[MU, s],
                    vx, y_roll(vx, 8), y_roll(vx, -1),
                    vy, y_roll(vy, -8), y_roll(vy, 1),
                    vz, y_roll(vz, -8), y_roll(vz, -1),
                )
                for i, gain in enumerate(gains):
                    strip[SXX + i, s] = strip[SXX + i, s] + gain


def sides(odd, inner, outer):
    even = odd[0] == 0

    def below(i, at):
        return jnp.where(even, outer[i][at], inner[i][at])

    def above(i, at):
        return jnp.where(even, inner[i][at], outer[i][at])

    return below, above


def full_kernel(
    layers, base, odd, vel, strs, lam, mu, buo, strips, lows, x_in, x_out, first_in, first_out, last_in, last_out, center,
    out_vel, out_strs, ext, state, strip,
):
    below, above = sides(odd, (x_in, first_in, last_in), (x_out, first_out, last_out))
    rest = layers - TOP
    water_borders(6 * rest, lows, below, above, center, ext)
    room = last_in.shape[0] - (UNITS - FIRST) * rest

    def units(side, unit):
        top = side(0, slice(6 * TOP + unit * TOP, 6 * TOP + unit * TOP + TOP))
        array, at = (1, base + unit * rest) if unit < FIRST else (2, room + (unit - FIRST) * rest)
        return (0, top), (TOP, side(array, slice(at, at + rest)))

    def rims(slot):
        top, low = slice(slot * TOP, slot * TOP + TOP), slice(slot * rest, (slot + 1) * rest)
        parts = (below(0, top), below(2, low)), (strips[top, :], lows[low, :]), (above(0, top), above(2, low))
        return [jnp.concatenate(p, axis=0) for p in parts]

    seismic(layers, (vel, strs, lam, mu, buo), rims, below, above, units, state, strip)
    for x in range(4):
        at = pl.ds(x, layers, stride=4)
        for f in range(3):
            out_vel[f, at, :] = state[f, 5 + x]
        for f in range(6):
            out_strs[f, at, :] = state[SXX + f, 5 + x]


def three_parts(value):
    high = value.astype(jnp.bfloat16)
    rest = value - high.astype(jnp.float32)
    middle = rest.astype(jnp.bfloat16)
    low = (rest - middle.astype(jnp.float32)).astype(jnp.bfloat16)
    return high, middle, low


def lift_kernel(
    grid_x, grid_y,
    odd, vel, strs, lam, mu, buo, strips, x_in, x_out, tiles, first_in, first_out, center, out, state, strip, lift,
):
    below, above = sides(odd, (x_in,), (x_out,))

    def units(side, unit):
        return ((0, side(0, slice((6 + unit) * TOP, (7 + unit) * TOP))),)

    def rims(slot):
        top = slice(slot * TOP, slot * TOP + TOP)
        return below(0, top), strips[top, :], above(0, top)

    seismic(TOP, (vel, strs, lam, mu, buo), rims, below, above, units, state, strip, lift)
    cols_dev = tiles.shape[1]
    wide = grid_y * cols_dev
    reach = grid_x * 8
    tile = tiles[...]
    tile_row, tile_col = tile // wide, tile % wide
    lead = lax.broadcasted_iota(jnp.int32, (reach, cols_dev), 0)
    wanted_row = jnp.where(lead % 8 < 6, lead // 8 * 4 - 1 + lead % 8, -2)
    column = lax.broadcasted_iota(jnp.int32, (wide, cols_dev), 0)
    edge = lax.broadcasted_iota(jnp.int32, (16, cols_dev), 0)
    wanted_edge = jnp.where(edge < 2 * grid_y, edge // 2 * cols_dev + jnp.where(edge % 2 == 0, -1, cols_dev), -2)
    contract = (((1,), (1,)), ((), ()))
    lefts, cols_hot, edges_hot = [], [], []
    for x in range(4):
        value = seismic_step * lift[x : x + 1, :]
        here = wanted_row == tile_row[x : x + 1, :]
        spread = jnp.where(here, jnp.broadcast_to(value, here.shape), 0.0)
        lefts.append(jnp.concatenate(three_parts(spread), axis=0))
        one = jnp.float32(1)
        cols_hot.append(jnp.where(column == tile_col[x : x + 1, :], one, 0.0).astype(jnp.bfloat16))
        edges_hot.append(jnp.where(wanted_edge == tile_col[x : x + 1, :], one, 0.0).astype(jnp.bfloat16))
    left = jnp.concatenate(lefts, axis=1)
    body = lax.dot_general(left, jnp.concatenate(cols_hot, axis=1), contract, preferred_element_type=jnp.float32)
    rim = lax.dot_general(jnp.concatenate(edges_hot, axis=1), left, contract, preferred_element_type=jnp.float32)
    body = body[:reach] + body[reach : 2 * reach] + body[2 * reach :]
    rim = rim[:, :reach] + rim[:, reach : 2 * reach] + rim[:, 2 * reach :]
    if reach < LANES:
        rim = jnp.concatenate([rim, jnp.zeros((16, LANES - reach), jnp.float32)], axis=1)
    row = rows_of((8, cols_dev))
    for gy in range(grid_y):
        beside = jnp.where(
            row == 6,
            jnp.broadcast_to(rim[2 * gy : 2 * gy + 1, :], (8, LANES)),
            jnp.broadcast_to(rim[2 * gy + 1 : 2 * gy + 2, :], (8, LANES)),
        )
        for gx in range(grid_x):
            block = body[gx * 8 : gx * 8 + 8, gy * cols_dev : (gy + 1) * cols_dev]
            out[gx * grid_y + gy] = jnp.where(row < 6, block, beside)


def center_kernel(surf, flow, depth, mask, ext):
    rows, cols = surf.shape
    ext[...] = jnp.zeros_like(ext)
    ext[0, 8 : 8 + rows, :cols] = surf[...]
    ext[1, 8 : 8 + rows, :cols] = flow[0]
    ext[2, 8 : 8 + rows, :cols] = flow[1]
    ext[3, 8 : 8 + rows, :cols] = depth[...] * mask[...].astype(jnp.float32)


def water_borders(low, lows, below, above, center, ext):
    tall, rows, cols = ext.shape[1], ext.shape[1] - 16, ext.shape[2] - LANES
    ext[...] = center[...]
    for f in range(4):
        for c in range(cols // LANES):
            row = slice(c * 8 + f * 2, c * 8 + f * 2 + 2)
            at = slice(c * LANES, (c + 1) * LANES)
            ext[f, 6:8, at] = below(1, row)
            ext[f, 8 + rows : 10 + rows, at] = above(1, row)
    rims = jnp.concatenate(
        [below(2, slice(low + rows - 8, low + rows)), lows[low : low + rows, :], above(2, slice(low, low + 8))], axis=0
    )
    wide_lane = lanes_of((tall, LANES))
    for f in range(4):
        after = pltpu.roll(rims, (-f * 32) % LANES, 1)
        before = pltpu.roll(rims, (96 - f * 32) % LANES, 1)
        ext[f, :, cols:] = jnp.where(wide_lane < 2, after, jnp.where(wide_lane >= LANES - 2, before, 0.0))


def water_kernel(grid_x, grid_y, place, parts, ext, out_surf, out_flow):
    rows, cols = out_surf.shape
    tall, wide = rows + 16, cols + LANES
    me_x, me_y = place[0], place[1]
    lift = jnp.sum(parts[...], axis=0)
    lane = lanes_of((8, LANES))
    spread = jnp.where(
        rows_of((LANES, cols)) == lanes_of((LANES, cols)) // 8, jnp.float32(1), 0.0
    ).astype(jnp.bfloat16)
    cells = jnp.dot(jnp.concatenate(three_parts(lift), axis=0), spread, preferred_element_type=jnp.float32)
    cells = cells[:8] + cells[8:16] + cells[16:]
    surface = []
    for r in range(tall // 8):
        picked = jnp.sum(jnp.where(lane == me_x * 8 + r, lift, 0.0), axis=1, keepdims=True)
        left = jnp.broadcast_to(picked[6:7, :], (8, LANES))
        right = jnp.broadcast_to(picked[7:8, :], (8, LANES))
        beside = jnp.where(lane < 2, right, jnp.where(lane >= LANES - 2, left, 0.0))
        lifted = jnp.concatenate([jnp.broadcast_to(cells[r : r + 1, :], (8, cols)), beside], axis=1)
        surface.append(ext[0, r * 8 : r * 8 + 8, :] + lifted)
    eta, u, w, carried = jnp.concatenate(surface, axis=0), ext[1], ext[2], ext[3]
    row, col = rows_of((tall, wide)), lanes_of((tall, wide))
    outside = jnp.logical_or(
        jnp.logical_and(me_x == grid_x - 1, row >= 8 + rows),
        jnp.logical_and(me_y == grid_y - 1, jnp.logical_and(col >= cols, col < cols + LANES // 2)),
    )
    for step in range(WATER_STEPS):
        u = u - water_step * (pltpu.roll(eta, tall - 1, 0) - eta)
        w = w - water_step * (pltpu.roll(eta, wide - 1, 1) - eta)
        cu, cw = carried * u, carried * w
        eta = eta - water_step * ((cu - pltpu.roll(cu, 1, 0)) + (cw - pltpu.roll(cw, 1, 1)))
        if step < WATER_STEPS - 1:
            eta = jnp.where(outside, 0.0, eta)
    out_surf[...] = eta[8 : 8 + rows, :cols]
    out_flow[0] = u[8 : 8 + rows, :cols]
    out_flow[1] = w[8 : 8 + rows, :cols]


def whole(shape):
    return pl.BlockSpec(shape, lambda i: (0,) * len(shape))


ANYWHERE = pl.BlockSpec(memory_space=pl.ANY)


class Fetch:
    def __init__(self, rows=None):
        self.rows = rows


def call(kernel, ins, in_specs, out_shapes, scratch=(), flops=0, same=(), vmem=VMEM):
    specs, fetched, cuts = [], [], {}
    for i, (a, s) in enumerate(zip(ins, in_specs)):
        if isinstance(s, Fetch):
            shape = a.shape if s.rows is None else a.shape[:-2] + (s.rows,) + a.shape[-1:]
            cuts[i] = len(fetched), shape
            fetched.append(pltpu.VMEM(shape, a.dtype))
            specs.append(pl.BlockSpec(memory_space=pltpu.HBM))
        else:
            specs.append(whole(a.shape) if s is None else s)
    count = len(ins)

    def fetching(*refs):
        refs = list(refs)
        arrived = refs.pop()
        buffers = refs[len(refs) - len(fetched) :]
        refs = refs[: len(refs) - len(fetched)]
        copies = []
        for i, (slot, shape) in cuts.items():
            source = refs[i]
            if shape != ins[i].shape:
                source = source.at[(slice(None),) * (len(shape) - 2) + (slice(0, shape[-2]),)]
            copies.append(pltpu.make_async_copy(source, buffers[slot], arrived.at[slot]))
            refs[i] = buffers[slot]
        for copy in copies:
            copy.start()
        for copy in copies:
            copy.wait()
        kernel(*refs)

    if cuts:
        scratch = list(scratch) + fetched + [pltpu.SemaphoreType.DMA((len(fetched),))]
    moved = sum(4 * a.size for a in ins) + sum(4 * math.prod(s.shape) for s in out_shapes)
    return pl.pallas_call(
        fetching if cuts else kernel,
        grid=(1,),
        in_specs=specs,
        out_specs=[ANYWHERE if i in dict(same).values() else whole(s.shape) for i, s in enumerate(out_shapes)],
        input_output_aliases=dict(same),
        out_shape=list(out_shapes),
        scratch_shapes=list(scratch),
        compiler_params=pltpu.CompilerParams(vmem_limit_bytes=vmem),
        cost_estimate=pl.CostEstimate(flops=flops, bytes_accessed=moved, transcendentals=0),
    )(*ins)


def shift(value, axis, by):
    count = lax.axis_size(axis)
    return lax.ppermute(value, axis, [(i, i + by) for i in range(count) if 0 <= i + by < count])


def partner(value, start):
    pairs = [(i, i + 1) for i in range(start, lax.axis_size("gx") - 1, 2)]
    return lax.ppermute(value, "gx", pairs + [(j, i) for i, j in pairs])


def f32(*shape):
    return jax.ShapeDtypeStruct(shape, jnp.float32)


def in_vmem(shape):
    return pltpu.VMEM(shape.shape, shape.dtype)


def body(
    velocity, stress, lame_lambda, shear_modulus, buoyancy, water_tile, water_surface, water_velocity, water_depth, wet_mask
):
    layers, rows_dev, cols_dev = lame_lambda.shape
    grid_x, grid_y = lax.axis_size("gx"), lax.axis_size("gy")
    devices = grid_x * grid_y
    water_rows, water_cols = water_surface.shape
    flat = layers * rows_dev
    own = (
        velocity.reshape(3, flat, cols_dev),
        stress.reshape(6, flat, cols_dev),
        lame_lambda.reshape(flat, cols_dev),
        shear_modulus.reshape(flat, cols_dev),
        buoyancy.reshape(flat, cols_dev),
    )
    water = (water_surface, water_velocity, water_depth, wet_mask)
    rest = layers - TOP
    water_tiles = water_cols // LANES * 8
    room = 6 * rest + water_rows
    x_shape = f32((6 + UNITS) * TOP, LANES)
    side_shape = f32(3 * layers + water_rows, LANES)
    near_shape = f32(UNITS * TOP, LANES)
    first_shape = f32(water_tiles + FIRST * rest, LANES)
    last_shape = f32(room + (UNITS - FIRST) * rest, LANES)
    place = jnp.stack([lax.axis_index("gx"), lax.axis_index("gy")]).astype(jnp.int32)
    odd = place[:1] % 2
    smem = pl.BlockSpec(memory_space=pltpu.SMEM)
    side, near_in, near_out, first_in, first_out, last_in, last_out = call(
        functools.partial(rows_kernel, layers),
        (odd,) + own + water,
        [smem] + [Fetch()] * 9,
        [in_vmem(side_shape), in_vmem(near_shape), in_vmem(near_shape), first_shape, first_shape, last_shape, last_shape],
        vmem=ALL_VMEM,
    )
    left, right = shift(side, "gy", 1), shift(side, "gy", -1)
    first_in, first_out = partner(first_in, 0), partner(first_out, 1)
    x_own, x_out, last_own, last_out = call(
        functools.partial(strip_kernel, layers),
        (left, right, side, near_in, near_out, last_in, last_out),
        [None] * 5 + [ANYWHERE] * 2,
        [in_vmem(x_shape), x_shape, last_shape, last_shape],
        [pltpu.VMEM((room, LANES), jnp.float32), pltpu.SemaphoreType.DMA((2,))],
        same=((5, 2), (6, 3)),
    )
    x_in, x_out = partner(x_own, 0), partner(x_out, 1)
    (last_out,) = call(
        after_kernel, (x_out, last_out), [ANYWHERE] * 2, [last_shape], same=((1, 0),)
    )
    last_in, last_out = partner(last_own, 0), partner(last_out, 1)
    ext_shape = f32(4, water_rows + 16, water_cols + LANES)
    (center,) = call(center_kernel, water, [None] * 4, [ext_shape])
    (send,) = call(
        functools.partial(lift_kernel, grid_x, grid_y),
        (odd,) + own + (x_own, x_in, x_out, water_tile, first_in, first_out, center),
        [smem] + [None] * 9 + [ANYWHERE] * 3,
        [in_vmem(f32(devices, 8, LANES))],
        [
            pltpu.VMEM((FIELDS, 14, TOP, LANES), jnp.float32),
            pltpu.VMEM((FIELDS, 2, TOP, LANES), jnp.float32),
            pltpu.VMEM((8, LANES), jnp.float32),
        ],
    )
    parts = lax.all_to_all(send, ("gx", "gy"), split_axis=0, concat_axis=0, tiled=True)
    final_velocity, final_stress, ext = call(
        functools.partial(full_kernel, layers, water_tiles),
        (odd,) + own + (x_own, last_own, x_in, x_out, first_in, first_out, last_in, last_out, center),
        [smem] + [Fetch()] * 6 + [Fetch(room)] + [Fetch()] * 7,
        [f32(3, flat, cols_dev), f32(6, flat, cols_dev), in_vmem(ext_shape)],
        [
            pltpu.VMEM((FIELDS, 14, layers, LANES), jnp.float32),
            pltpu.VMEM((FIELDS, 2, layers, LANES), jnp.float32),
        ],
        flops=70 * 9 * flat * cols_dev * 4,
        vmem=58 * 1024 * 1024,
    )
    final_surface, final_flow = call(
        functools.partial(water_kernel, grid_x, grid_y),
        (place, parts, ext),
        [smem, None, None],
        [f32(water_rows, water_cols), f32(2, water_rows, water_cols)],
    )
    return (
        final_velocity.reshape(velocity.shape),
        final_stress.reshape(stress.shape),
        final_surface,
        final_flow,
    )


def solution(mesh):
    placed = (
        P(None, None, "gx", "gy"),
        P(None, None, "gx", "gy"),
        P(None, "gx", "gy"),
        P(None, "gx", "gy"),
        P(None, "gx", "gy"),
        P("gx", "gy"),
        P("gx", "gy"),
        P(None, "gx", "gy"),
        P("gx", "gy"),
        P("gx", "gy"),
    )
    return jax.shard_map(
        body,
        mesh=mesh,
        in_specs=placed,
        out_specs=(
            P(None, None, "gx", "gy"),
            P(None, None, "gx", "gy"),
            P("gx", "gy"),
            P(None, "gx", "gy"),
        ),
        check_vma=False,
    )
```

```python
import functools
import math

import jax
import jax.numpy as jnp
from jax import lax
from jax.experimental import pallas as pl
from jax.experimental.pallas import tpu as pltpu
from jax.sharding import PartitionSpec as P

SEIS_STEPS = 4
WATER_STEPS = 2

seismic_step = 0.15
water_step = 0.4

VX, VY, VZ, SXX, SYY, SZZ, SXY, SXZ, SYZ, LAM, MU, BUO = range(12)
FIELDS = 12
LANES = 128
FAR_BELOW = (VX, SXX, SXY, SXZ, BUO)
FAR_ABOVE = (VY, VZ, SXX, SYY, SZZ, SXY, SXZ, SYZ, BUO)
UP_UNITS = [(f, x) for x in (1, 2, 3) for f in range(FIELDS)] + [(f, 0) for f in (SXY, SXZ, VX, SXX, BUO)]
DOWN_UNITS = [(f, x) for x in range(4) for f in (FAR_ABOVE if x == 3 else range(FIELDS))]
NEAR = 38
FIRST = 19
UNITS = max(len(UP_UNITS), len(DOWN_UNITS))
VMEM = 48 * 1024 * 1024
ALL_VMEM = 63 * 1024 * 1024
TOP = 8


def lanes_of(shape):
    return lax.broadcasted_iota(jnp.int32, shape, len(shape) - 1)


def rows_of(shape):
    return lax.broadcasted_iota(jnp.int32, shape, len(shape) - 2)


def own_row(refs, field, x, layers):
    vel, strs, lam, mu, buo = refs
    at = pl.ds(x, layers, stride=4)
    if field < 3:
        return vel[field, at, :]
    if field < 9:
        return strs[field - 3, at, :]
    return (lam, mu, buo)[field - 9][at, :]


def side_kernel(layers, vel, strs, lam, mu, buo, surf, flow, depth, mask, side):
    refs = (vel, strs, lam, mu, buo)
    lane = lanes_of((layers, LANES))
    for tile in range(3):
        packed = jnp.zeros((layers, LANES), jnp.float32)
        for q in range(4):
            for x in range(4):
                row = own_row(refs, tile * 4 + q, x, layers)
                group = q * 4 + x
                packed = jnp.where(lane // 8 == group, pltpu.roll(row, (group * 8 + 4) % LANES, 1), packed)
        side[tile * layers : (tile + 1) * layers, :] = packed
    rows, cols = surf.shape
    lane = lanes_of((rows, LANES))
    packed = jnp.zeros((rows, LANES), jnp.float32)
    for f in range(4):
        first = pltpu.roll(water_part(f, surf, flow, depth, mask, 0, rows, 0, LANES), f * 32, 1)
        last = pltpu.roll(water_part(f, surf, flow, depth, mask, 0, rows, cols - LANES, cols), (f * 32 + 32) % LANES, 1)
        packed = jnp.where(lane // 2 == f * 16, first, packed)
        packed = jnp.where(lane // 2 == f * 16 + 15, last, packed)
    side[3 * layers :, :] = packed


def water_part(f, surf, flow, depth, mask, r0, r1, c0, c1):
    if f == 0:
        return surf[r0:r1, c0:c1]
    if f < 3:
        return flow[f - 1, r0:r1, c0:c1]
    return depth[r0:r1, c0:c1] * mask[r0:r1, c0:c1].astype(jnp.float32)


def rows_kernel(
    layers, odd, vel, strs, lam, mu, buo, surf, flow, depth, mask,
    side, near_in, near_out, first_in, first_out, last_in, last_out,
):
    refs = (vel, strs, lam, mu, buo)
    rows, cols = surf.shape
    base = cols // LANES * 8
    rest = layers - TOP
    room = last_in.shape[0] - (UNITS - FIRST) * rest - (UNITS - NEAR) * TOP
    tops = room + (UNITS - FIRST) * rest

    side_kernel(layers, vel, strs, lam, mu, buo, surf, flow, depth, mask, side)

    def write(units, start, near, first, last):
        for f in range(4):
            for c in range(cols // LANES):
                first[c * 8 + f * 2 : c * 8 + f * 2 + 2, :] = water_part(
                    f, surf, flow, depth, mask, start, start + 2, c * LANES, (c + 1) * LANES
                )
        for unit, (field, x) in enumerate(units):
            row = own_row(refs, field, x, layers)
            if unit < NEAR:
                near[unit * TOP : unit * TOP + TOP, :] = row[:TOP]
            else:
                last[tops + (unit - NEAR) * TOP : tops + (unit - NEAR + 1) * TOP, :] = row[:TOP]
            if unit < FIRST:
                first[base + unit * rest : base + (unit + 1) * rest, :] = row[TOP:]
            else:
                last[room + (unit - FIRST) * rest : room + (unit - FIRST + 1) * rest, :] = row[TOP:]

    @pl.when(odd[0] == 0)
    def _():
        write(UP_UNITS, rows - 2, near_in, first_in, last_in)
        write(DOWN_UNITS, 0, near_out, first_out, last_out)

    @pl.when(odd[0] == 1)
    def _():
        write(UP_UNITS, rows - 2, near_out, first_out, last_out)
        write(DOWN_UNITS, 0, near_in, first_in, last_in)


def strip_kernel(
    layers, left, right, own, near_in, near_out, last_in, last_out, x_in, x_out, same_in, same_out, low, done
):
    rest = layers - TOP
    seis = 3 * layers
    inner = lanes_of((layers, LANES)) % 8 < 4
    for tile in range(3):
        at = slice(tile * layers, (tile + 1) * layers)
        mine = own[at, :]
        for edge, rim in ((0, jnp.where(inner, left[at, :], mine)), (1, jnp.where(inner, mine, right[at, :]))):
            slot = edge * 3 + tile
            low[slot * rest : (slot + 1) * rest, :] = rim[TOP:]
            for x_ref in (x_in, x_out):
                x_ref[slot * TOP : slot * TOP + TOP, :] = rim[:TOP]
    rows = own.shape[0] - seis
    low[6 * rest :, :] = jnp.where(lanes_of((rows, LANES)) % 32 < 16, right[seis:, :], left[seis:, :])
    copies = [
        pltpu.make_async_copy(low, same.at[0 : low.shape[0], :], done.at[i]) for i, same in enumerate((same_in, same_out))
    ]
    for copy in copies:
        copy.start()
    x_in[6 * TOP :, :] = near_in[...]
    x_out[6 * TOP :, :] = near_out[...]
    for copy in copies:
        copy.wait()


def after_kernel(first, second, last, same):
    pass


def z_forward(f):
    n = f.shape[0]
    beyond = jnp.where(rows_of(f.shape) == n - 1, 0.0, pltpu.roll(f, n - 1, 0))
    return beyond - f


def z_backward(f):
    before = jnp.where(rows_of(f.shape) == 0, 0.0, pltpu.roll(f, 1, 0))
    return f - before


def new_velocity(vx, vy, vz, hb, sxx, sxx_xp, syy, syy_yp, szz, sxy, sxy_xm, sxy_ym, sxz, sxz_xm, syz, syz_ym):
    vx = vx + hb * ((sxx_xp - sxx) + (sxy - sxy_ym) + z_backward(sxz))
    vy = vy + hb * ((sxy - sxy_xm) + (syy_yp - syy) + z_backward(syz))
    vz = vz + hb * ((sxz - sxz_xm) + (syz - syz_ym) + z_forward(szz))
    return vx, vy, vz


def stress_gain(hl, hm, vx, vx_xm, vx_yp, vy, vy_xp, vy_ym, vz, vz_xp, vz_yp):
    ex = vx - vx_xm
    ey = vy - vy_ym
    ez = z_backward(vz)
    d = hl * (ex + ey + ez)
    twice = hm + hm
    return (
        d + twice * ex,
        d + twice * ey,
        d + twice * ez,
        hm * ((vx_yp - vx) + (vy_xp - vy)),
        hm * (z_forward(vx) + (vz_xp - vz)),
        hm * (z_forward(vy) + (vz_yp - vz)),
    )


def seismic(layers, refs, rims, below, above, units, state, strip, lift=None):
    lane = lanes_of((layers, LANES))

    def scaled(field, value):
        return value * seismic_step if field >= LAM else value

    for field in range(FIELDS):
        for x in range(4):
            state[field, 5 + x] = scaled(field, own_row(refs, field, x, layers))
    up_at = {unit: i for i, unit in enumerate(UP_UNITS)}
    down_at = {unit: i for i, unit in enumerate(DOWN_UNITS)}
    zero = jnp.zeros((layers, LANES), jnp.float32)
    for field in range(FIELDS):
        state[field, 0] = zero
        state[field, 13] = zero
        for x in range(4):
            for at, side, first in ((up_at, below, 1), (down_at, above, 9)):
                if (field, x) not in at:
                    state[field, first + x] = zero
                    continue
                for layer, piece in units(side, at[field, x]):
                    state[field, first + x, layer : layer + piece.shape[0]] = scaled(field, piece)
        tile, q = field // 4, field % 4
        for s in range(2):
            low, own, high = rims(s * 3 + tile)
            value = jnp.where(
                lane < 32,
                pltpu.roll(low, (-q * 32) % LANES, 1),
                jnp.where(
                    lane < 64,
                    pltpu.roll(own, (32 - q * 32) % LANES, 1),
                    jnp.where(lane < 96, pltpu.roll(high, (64 - q * 32) % LANES, 1), 0.0),
                ),
            )
            strip[field, s] = scaled(field, value)

    if lift is not None:
        lift[...] = jnp.zeros_like(lift)

    def y_plus(field, value, row):
        rim = pltpu.roll(strip[field, 1], LANES - 5 - row * 8, 1)
        return jnp.where(lane == LANES - 1, rim, pltpu.roll(value, LANES - 1, 1))

    def y_minus(field, value, row):
        rim = pltpu.roll(strip[field, 0], LANES - 3 - row * 8, 1)
        return jnp.where(lane == 0, rim, pltpu.roll(value, 1, 1))

    def velocity_row(row):
        at = row + 1
        sxx, syy, szz, sxy, sxz, syz = [state[f, at] for f in (SXX, SYY, SZZ, SXY, SXZ, SYZ)]
        vx, vy, vz = new_velocity(
            state[VX, at], state[VY, at], state[VZ, at], state[BUO, at],
            sxx, state[SXX, at + 1], syy, y_plus(SYY, syy, row), szz,
            sxy, state[SXY, at - 1], y_minus(SXY, sxy, row),
            sxz, state[SXZ, at - 1], syz, y_minus(SYZ, syz, row),
        )
        state[VX, at] = vx
        state[VY, at] = vy
        state[VZ, at] = vz

    def stress_row(row):
        at = row + 1
        vx, vy, vz = state[VX, at], state[VY, at], state[VZ, at]
        gains = stress_gain(
            state[LAM, at], state[MU, at],
            vx, state[VX, at - 1], y_plus(VX, vx, row),
            vy, state[VY, at + 1], y_minus(VY, vy, row),
            vz, state[VZ, at + 1], y_plus(VZ, vz, row),
        )
        for i, gain in enumerate(gains):
            state[SXX + i, at] = state[SXX + i, at] + gain

    def each(first, end, update):
        for row in range(first, end):
            update(row)

    def y_roll(value, by):
        return pltpu.roll(value, by % LANES, 1)

    for step in range(SEIS_STEPS):
        last = step == SEIS_STEPS - 1
        if last and lift is not None:
            each(4, 8, velocity_row)
        else:
            each(step, 12 - step, velocity_row)
            for s in range(2):
                sxx, syy, szz, sxy, sxz, syz = [strip[f, s] for f in (SXX, SYY, SZZ, SXY, SXZ, SYZ)]
                new = new_velocity(
                    strip[VX, s], strip[VY, s], strip[VZ, s], strip[BUO, s],
                    sxx, y_roll(sxx, -8), syy, y_roll(syy, -1), szz,
                    sxy, y_roll(sxy, 8), y_roll(sxy, 1),
                    sxz, y_roll(sxz, 8), syz, y_roll(syz, 1),
                )
                for i in range(3):
                    strip[VX + i, s] = new[i]
        if lift is not None:
            for x in range(4):
                lift[x : x + 1, :] = lift[x : x + 1, :] + state[VZ, 5 + x, 0:1, :]
        if last and lift is not None:
            break
        each(step + 1, 11 - step, stress_row)
        if not last:
            for s in range(2):
                vx, vy, vz = strip[VX, s], strip[VY, s], strip[VZ, s]
                gains = stress_gain(
                    strip[LAM, s], strip[MU, s],
                    vx, y_roll(vx, 8), y_roll(vx, -1),
                    vy, y_roll(vy, -8), y_roll(vy, 1),
                    vz, y_roll(vz, -8), y_roll(vz, -1),
                )
                for i, gain in enumerate(gains):
                    strip[SXX + i, s] = strip[SXX + i, s] + gain


def sides(odd, inner, outer):
    even = odd[0] == 0

    def below(i, at):
        return jnp.where(even, outer[i][at], inner[i][at])

    def above(i, at):
        return jnp.where(even, inner[i][at], outer[i][at])

    return below, above


def full_kernel(
    layers, base, odd, vel, strs, lam, mu, buo, strips, lows, x_in, x_out, first_in, first_out, last_in, last_out, center,
    out_vel, out_strs, ext, state, strip,
):
    below, above = sides(odd, (x_in, first_in, last_in), (x_out, first_out, last_out))
    rest = layers - TOP
    water_borders(6 * rest, lows, below, above, center, ext)
    room = last_in.shape[0] - (UNITS - FIRST) * rest - (UNITS - NEAR) * TOP
    tops = room + (UNITS - FIRST) * rest

    def units(side, unit):
        array, at = (0, 6 * TOP + unit * TOP) if unit < NEAR else (2, tops + (unit - NEAR) * TOP)
        top = side(array, slice(at, at + TOP))
        array, at = (1, base + unit * rest) if unit < FIRST else (2, room + (unit - FIRST) * rest)
        return (0, top), (TOP, side(array, slice(at, at + rest)))

    def rims(slot):
        top, low = slice(slot * TOP, slot * TOP + TOP), slice(slot * rest, (slot + 1) * rest)
        parts = (below(0, top), below(2, low)), (strips[top, :], lows[low, :]), (above(0, top), above(2, low))
        return [jnp.concatenate(p, axis=0) for p in parts]

    seismic(layers, (vel, strs, lam, mu, buo), rims, below, above, units, state, strip)
    for x in range(4):
        at = pl.ds(x, layers, stride=4)
        for f in range(3):
            out_vel[f, at, :] = state[f, 5 + x]
        for f in range(6):
            out_strs[f, at, :] = state[SXX + f, 5 + x]


def three_parts(value):
    high = value.astype(jnp.bfloat16)
    rest = value - high.astype(jnp.float32)
    middle = rest.astype(jnp.bfloat16)
    low = (rest - middle.astype(jnp.float32)).astype(jnp.bfloat16)
    return high, middle, low


def lift_kernel(
    grid_x, grid_y,
    odd, vel, strs, lam, mu, buo, strips, x_in, x_out, tiles, first_in, first_out, center, out, state, strip, lift,
):
    below, above = sides(odd, (x_in,), (x_out,))

    def units(side, unit):
        if unit >= NEAR:
            return ((0, jnp.zeros((TOP, LANES), jnp.float32)),)
        return ((0, side(0, slice((6 + unit) * TOP, (7 + unit) * TOP))),)

    def rims(slot):
        top = slice(slot * TOP, slot * TOP + TOP)
        return below(0, top), strips[top, :], above(0, top)

    seismic(TOP, (vel, strs, lam, mu, buo), rims, below, above, units, state, strip, lift)
    cols_dev = tiles.shape[1]
    wide = grid_y * cols_dev
    reach = grid_x * 8
    tile = tiles[...]
    tile_row, tile_col = tile // wide, tile % wide
    lead = lax.broadcasted_iota(jnp.int32, (reach, cols_dev), 0)
    wanted_row = jnp.where(lead % 8 < 6, lead // 8 * 4 - 1 + lead % 8, -2)
    column = lax.broadcasted_iota(jnp.int32, (wide, cols_dev), 0)
    edge = lax.broadcasted_iota(jnp.int32, (16, cols_dev), 0)
    wanted_edge = jnp.where(edge < 2 * grid_y, edge // 2 * cols_dev + jnp.where(edge % 2 == 0, -1, cols_dev), -2)
    contract = (((1,), (1,)), ((), ()))
    lefts, cols_hot, edges_hot = [], [], []
    for x in range(4):
        value = seismic_step * lift[x : x + 1, :]
        here = wanted_row == tile_row[x : x + 1, :]
        spread = jnp.where(here, jnp.broadcast_to(value, here.shape), 0.0)
        lefts.append(jnp.concatenate(three_parts(spread), axis=0))
        one = jnp.float32(1)
        cols_hot.append(jnp.where(column == tile_col[x : x + 1, :], one, 0.0).astype(jnp.bfloat16))
        edges_hot.append(jnp.where(wanted_edge == tile_col[x : x + 1, :], one, 0.0).astype(jnp.bfloat16))
    left = jnp.concatenate(lefts, axis=1)
    body = lax.dot_general(left, jnp.concatenate(cols_hot, axis=1), contract, preferred_element_type=jnp.float32)
    rim = lax.dot_general(jnp.concatenate(edges_hot, axis=1), left, contract, preferred_element_type=jnp.float32)
    body = body[:reach] + body[reach : 2 * reach] + body[2 * reach :]
    rim = rim[:, :reach] + rim[:, reach : 2 * reach] + rim[:, 2 * reach :]
    if reach < LANES:
        rim = jnp.concatenate([rim, jnp.zeros((16, LANES - reach), jnp.float32)], axis=1)
    row = rows_of((8, cols_dev))
    for gy in range(grid_y):
        beside = jnp.where(
            row == 6,
            jnp.broadcast_to(rim[2 * gy : 2 * gy + 1, :], (8, LANES)),
            jnp.broadcast_to(rim[2 * gy + 1 : 2 * gy + 2, :], (8, LANES)),
        )
        for gx in range(grid_x):
            block = body[gx * 8 : gx * 8 + 8, gy * cols_dev : (gy + 1) * cols_dev]
            out[gx * grid_y + gy] = jnp.where(row < 6, block, beside)


def center_kernel(surf, flow, depth, mask, ext):
    rows, cols = surf.shape
    ext[...] = jnp.zeros_like(ext)
    ext[0, 8 : 8 + rows, :cols] = surf[...]
    ext[1, 8 : 8 + rows, :cols] = flow[0]
    ext[2, 8 : 8 + rows, :cols] = flow[1]
    ext[3, 8 : 8 + rows, :cols] = depth[...] * mask[...].astype(jnp.float32)


def water_borders(low, lows, below, above, center, ext):
    tall, rows, cols = ext.shape[1], ext.shape[1] - 16, ext.shape[2] - LANES
    ext[...] = center[...]
    for f in range(4):
        for c in range(cols // LANES):
            row = slice(c * 8 + f * 2, c * 8 + f * 2 + 2)
            at = slice(c * LANES, (c + 1) * LANES)
            ext[f, 6:8, at] = below(1, row)
            ext[f, 8 + rows : 10 + rows, at] = above(1, row)
    rims = jnp.concatenate(
        [below(2, slice(low + rows - 8, low + rows)), lows[low : low + rows, :], above(2, slice(low, low + 8))], axis=0
    )
    wide_lane = lanes_of((tall, LANES))
    for f in range(4):
        after = pltpu.roll(rims, (-f * 32) % LANES, 1)
        before = pltpu.roll(rims, (96 - f * 32) % LANES, 1)
        ext[f, :, cols:] = jnp.where(wide_lane < 2, after, jnp.where(wide_lane >= LANES - 2, before, 0.0))


def water_kernel(grid_x, grid_y, place, parts, ext, out_surf, out_flow):
    rows, cols = out_surf.shape
    tall, wide = rows + 16, cols + LANES
    me_x, me_y = place[0], place[1]
    lift = jnp.sum(parts[...], axis=0)
    lane = lanes_of((8, LANES))
    spread = jnp.where(
        rows_of((LANES, cols)) == lanes_of((LANES, cols)) // 8, jnp.float32(1), 0.0
    ).astype(jnp.bfloat16)
    cells = jnp.dot(jnp.concatenate(three_parts(lift), axis=0), spread, preferred_element_type=jnp.float32)
    cells = cells[:8] + cells[8:16] + cells[16:]
    surface = []
    for r in range(tall // 8):
        picked = jnp.sum(jnp.where(lane == me_x * 8 + r, lift, 0.0), axis=1, keepdims=True)
        left = jnp.broadcast_to(picked[6:7, :], (8, LANES))
        right = jnp.broadcast_to(picked[7:8, :], (8, LANES))
        beside = jnp.where(lane < 2, right, jnp.where(lane >= LANES - 2, left, 0.0))
        lifted = jnp.concatenate([jnp.broadcast_to(cells[r : r + 1, :], (8, cols)), beside], axis=1)
        surface.append(ext[0, r * 8 : r * 8 + 8, :] + lifted)
    eta, u, w, carried = jnp.concatenate(surface, axis=0), ext[1], ext[2], ext[3]
    row, col = rows_of((tall, wide)), lanes_of((tall, wide))
    outside = jnp.logical_or(
        jnp.logical_and(me_x == grid_x - 1, row >= 8 + rows),
        jnp.logical_and(me_y == grid_y - 1, jnp.logical_and(col >= cols, col < cols + LANES // 2)),
    )
    for step in range(WATER_STEPS):
        u = u - water_step * (pltpu.roll(eta, tall - 1, 0) - eta)
        w = w - water_step * (pltpu.roll(eta, wide - 1, 1) - eta)
        cu, cw = carried * u, carried * w
        eta = eta - water_step * ((cu - pltpu.roll(cu, 1, 0)) + (cw - pltpu.roll(cw, 1, 1)))
        if step < WATER_STEPS - 1:
            eta = jnp.where(outside, 0.0, eta)
    out_surf[...] = eta[8 : 8 + rows, :cols]
    out_flow[0] = u[8 : 8 + rows, :cols]
    out_flow[1] = w[8 : 8 + rows, :cols]


def whole(shape):
    return pl.BlockSpec(shape, lambda i: (0,) * len(shape))


ANYWHERE = pl.BlockSpec(memory_space=pl.ANY)


class Fetch:
    def __init__(self, rows=None):
        self.rows = rows


def call(kernel, ins, in_specs, out_shapes, scratch=(), flops=0, same=(), vmem=VMEM):
    specs, fetched, cuts = [], [], {}
    for i, (a, s) in enumerate(zip(ins, in_specs)):
        if isinstance(s, Fetch):
            shape = a.shape if s.rows is None else a.shape[:-2] + (s.rows,) + a.shape[-1:]
            cuts[i] = len(fetched), shape
            fetched.append(pltpu.VMEM(shape, a.dtype))
            specs.append(pl.BlockSpec(memory_space=pltpu.HBM))
        else:
            specs.append(whole(a.shape) if s is None else s)
    count = len(ins)

    def fetching(*refs):
        refs = list(refs)
        arrived = refs.pop()
        buffers = refs[len(refs) - len(fetched) :]
        refs = refs[: len(refs) - len(fetched)]
        copies = []
        for i, (slot, shape) in cuts.items():
            source = refs[i]
            if shape != ins[i].shape:
                source = source.at[(slice(None),) * (len(shape) - 2) + (slice(0, shape[-2]),)]
            copies.append(pltpu.make_async_copy(source, buffers[slot], arrived.at[slot]))
            refs[i] = buffers[slot]
        for copy in copies:
            copy.start()
        for copy in copies:
            copy.wait()
        kernel(*refs)

    if cuts:
        scratch = list(scratch) + fetched + [pltpu.SemaphoreType.DMA((len(fetched),))]
    moved = sum(4 * a.size for a in ins) + sum(4 * math.prod(s.shape) for s in out_shapes)
    return pl.pallas_call(
        fetching if cuts else kernel,
        grid=(1,),
        in_specs=specs,
        out_specs=[ANYWHERE if i in dict(same).values() else whole(s.shape) for i, s in enumerate(out_shapes)],
        input_output_aliases=dict(same),
        out_shape=list(out_shapes),
        scratch_shapes=list(scratch),
        compiler_params=pltpu.CompilerParams(vmem_limit_bytes=vmem),
        cost_estimate=pl.CostEstimate(flops=flops, bytes_accessed=moved, transcendentals=0),
    )(*ins)


def shift(value, axis, by):
    count = lax.axis_size(axis)
    return lax.ppermute(value, axis, [(i, i + by) for i in range(count) if 0 <= i + by < count])


def partner(value, start):
    pairs = [(i, i + 1) for i in range(start, lax.axis_size("gx") - 1, 2)]
    return lax.ppermute(value, "gx", pairs + [(j, i) for i, j in pairs])


def f32(*shape):
    return jax.ShapeDtypeStruct(shape, jnp.float32)


def in_vmem(shape):
    return pltpu.VMEM(shape.shape, shape.dtype)


def body(
    velocity, stress, lame_lambda, shear_modulus, buoyancy, water_tile, water_surface, water_velocity, water_depth, wet_mask
):
    layers, rows_dev, cols_dev = lame_lambda.shape
    grid_x, grid_y = lax.axis_size("gx"), lax.axis_size("gy")
    devices = grid_x * grid_y
    water_rows, water_cols = water_surface.shape
    flat = layers * rows_dev
    own = (
        velocity.reshape(3, flat, cols_dev),
        stress.reshape(6, flat, cols_dev),
        lame_lambda.reshape(flat, cols_dev),
        shear_modulus.reshape(flat, cols_dev),
        buoyancy.reshape(flat, cols_dev),
    )
    water = (water_surface, water_velocity, water_depth, wet_mask)
    rest = layers - TOP
    water_tiles = water_cols // LANES * 8
    room = 6 * rest + water_rows
    x_shape = f32((6 + NEAR) * TOP, LANES)
    side_shape = f32(3 * layers + water_rows, LANES)
    near_shape = f32(NEAR * TOP, LANES)
    first_shape = f32(water_tiles + FIRST * rest, LANES)
    last_shape = f32(room + (UNITS - FIRST) * rest + (UNITS - NEAR) * TOP, LANES)
    place = jnp.stack([lax.axis_index("gx"), lax.axis_index("gy")]).astype(jnp.int32)
    odd = place[:1] % 2
    smem = pl.BlockSpec(memory_space=pltpu.SMEM)
    side, near_in, near_out, first_in, first_out, last_in, last_out = call(
        functools.partial(rows_kernel, layers),
        (odd,) + own + water,
        [smem] + [Fetch()] * 9,
        [in_vmem(side_shape), in_vmem(near_shape), in_vmem(near_shape), first_shape, first_shape, last_shape, last_shape],
        vmem=ALL_VMEM,
    )
    left, right = shift(side, "gy", 1), shift(side, "gy", -1)
    first_in, first_out = partner(first_in, 0), partner(first_out, 1)
    x_own, x_out, last_own, last_out = call(
        functools.partial(strip_kernel, layers),
        (left, right, side, near_in, near_out, last_in, last_out),
        [None] * 5 + [ANYWHERE] * 2,
        [in_vmem(x_shape), x_shape, last_shape, last_shape],
        [pltpu.VMEM((room, LANES), jnp.float32), pltpu.SemaphoreType.DMA((2,))],
        same=((5, 2), (6, 3)),
    )
    x_in, x_out = partner(x_own, 0), partner(x_out, 1)
    (last_out,) = call(
        after_kernel, (x_out, x_in, last_out), [ANYWHERE] * 3, [last_shape], same=((2, 0),)
    )
    last_in, last_out = partner(last_own, 0), partner(last_out, 1)
    ext_shape = f32(4, water_rows + 16, water_cols + LANES)
    (center,) = call(center_kernel, water, [None] * 4, [ext_shape])
    (send,) = call(
        functools.partial(lift_kernel, grid_x, grid_y),
        (odd,) + own + (x_own, x_in, x_out, water_tile, first_in, first_out, center),
        [smem] + [None] * 9 + [ANYWHERE] * 3,
        [in_vmem(f32(devices, 8, LANES))],
        [
            pltpu.VMEM((FIELDS, 14, TOP, LANES), jnp.float32),
            pltpu.VMEM((FIELDS, 2, TOP, LANES), jnp.float32),
            pltpu.VMEM((8, LANES), jnp.float32),
        ],
    )
    parts = lax.all_to_all(send, ("gx", "gy"), split_axis=0, concat_axis=0, tiled=True)
    final_velocity, final_stress, ext = call(
        functools.partial(full_kernel, layers, water_tiles),
        (odd,) + own + (x_own, last_own, x_in, x_out, first_in, first_out, last_in, last_out, center),
        [smem] + [Fetch()] * 6 + [Fetch(room)] + [Fetch()] * 7,
        [f32(3, flat, cols_dev), f32(6, flat, cols_dev), in_vmem(ext_shape)],
        [
            pltpu.VMEM((FIELDS, 14, layers, LANES), jnp.float32),
            pltpu.VMEM((FIELDS, 2, layers, LANES), jnp.float32),
        ],
        flops=70 * 9 * flat * cols_dev * 4,
        vmem=58 * 1024 * 1024,
    )
    final_surface, final_flow = call(
        functools.partial(water_kernel, grid_x, grid_y),
        (place, parts, ext),
        [smem, None, None],
        [f32(water_rows, water_cols), f32(2, water_rows, water_cols)],
    )
    return (
        final_velocity.reshape(velocity.shape),
        final_stress.reshape(stress.shape),
        final_surface,
        final_flow,
    )


def solution(mesh):
    placed = (
        P(None, None, "gx", "gy"),
        P(None, None, "gx", "gy"),
        P(None, "gx", "gy"),
        P(None, "gx", "gy"),
        P(None, "gx", "gy"),
        P("gx", "gy"),
        P("gx", "gy"),
        P(None, "gx", "gy"),
        P("gx", "gy"),
        P("gx", "gy"),
    )
    return jax.shard_map(
        body,
        mesh=mesh,
        in_specs=placed,
        out_specs=(
            P(None, None, "gx", "gy"),
            P(None, None, "gx", "gy"),
            P("gx", "gy"),
            P(None, "gx", "gy"),
        ),
        check_vma=False,
    )
```
